256 devices in a mesh: scene: 4 (over x), dom: 64 (over z, y, core).
Axes of the slice: x: 4, y: 4, z: 8, core: 2. Of those that a mesh axis runs over, the one named last changes fastest.
Arguments:
- features: bfloat16 [2048, 64, 512], P(('scene', 'dom')), parts along dimension 0, may hold values from -6 to 6
- cotangent: bfloat16 [2048, 64, 512], P(('scene', 'dom')), parts along dimension 0, may hold values from -6 to 6
- weight: bfloat16 [27, 64, 64], replicated, may hold values from -0.15625 to 0.15625
- mask_words: int32 [2048, 18], P(('scene', 'dom')), parts along dimension 0, may hold values from 0 to 1073741823, as said below
- neighbors: int32 [2048, 26], P(('scene', 'dom')), parts along dimension 0, may hold values from -1 to 511, as said below
Outputs:
- out_features: bfloat16 [2048, 64, 512], P(('scene', 'dom')), parts along dimension 0
- in_grad: bfloat16 [2048, 64, 512], P(('scene', 'dom')), parts along dimension 0
- weight_grad: float32 [108, 64, 64], P('scene'), parts along dimension 0
The draws below stay inside these ranges and needn't reach their ends.
There are 4 independent parts, one for each index of `scene`. The reference program is written for one: setup_inputs(seed, part) draws one part's arguments, and reference() takes and returns one part's arrays. A program takes and returns all parts, laid end to end along the dimension named above; an argument that names none is the same for every part. Nothing has to cross between parts.
Inputs may be any that keep to these rules, and one draw needn't show every extreme that they name: `mask_words`: bit r of word w is voxel 30 w + r of the leaf; bits at or past 512 are 0; unused slots have all bits 0. An id is owner * 8 + slot, owner being the index along dom. All leaves at one leaf position along the first dimension have the same owner; a neighbor at first offset -1 is owned by the same device or the one below it, at +1 by the same device or the one above it. The table is symmetric: b is listed as a neighbor of a at offset (p, q, r) exactly when a is listed for b at (-p, -q, -r). Used slots of a device come first; unused slots list no neighbors. At most 4 leaves of one device have a neighbor owned by one given adjacent device, and some device reaches that in every draw; some device uses all 8 slots in every draw.
All inputs are finite; a program needn't handle non-finite values.
Results may differ from the reference program's by a relative error of at most 0.001.
Values may be sent and summed in bfloat16 or wider, within the bound.
A program may use at most 256 MiB of HBM per device.

```python
import jax
import jax.numpy as jnp
from jax import lax

C = 64
LEAF = 8
LEAF_DEV = 8
PLANES = 4
CROSS_Y = 4
CROSS_Z = 1
VOXELS = 512
MASK_WORDS = 18
SLOTS = 512


def leaf_layout(key):
    devices = SLOTS // LEAF_DEV
    cross_cells = CROSS_Y * CROSS_Z
    positions = PLANES * cross_cells
    key_full, key_count, key_rank = jax.random.split(jax.random.fold_in(key, 17), 3)
    full_device = jax.random.randint(key_full, (), 0, devices - 1)
    device_ids = jnp.arange(devices, dtype=jnp.int32)
    place_ids = jnp.arange(positions, dtype=jnp.int32)
    plane_of = place_ids // cross_cells
    counts = jax.random.randint(key_count, (devices,), LEAF_DEV // 4, LEAF_DEV + 1)
    counts = jnp.where(device_ids == full_device, LEAF_DEV, counts)
    counts = jnp.where(device_ids == full_device + 1, jnp.maximum(counts, cross_cells), counts)
    forced_full = (device_ids[:, None] == full_device) & (plane_of[None, :] >= PLANES - 2)
    forced_next = (device_ids[:, None] == full_device + 1) & (plane_of[None, :] == 0)
    forced = forced_full | forced_next
    scores = jax.random.randint(key_rank, (devices, positions), 0, 1 << 20) * positions + place_ids[None, :]
    scores = jnp.where(forced, place_ids[None, :] - positions, scores)
    sorting = jnp.argsort(scores, axis=1)
    rank_table = jnp.argsort(sorting, axis=1)
    occupied = rank_table < counts[:, None]
    slot_of = jnp.where(occupied, jnp.cumsum(occupied.astype(jnp.int32), axis=1) - 1, -1)
    place_key = jnp.where(occupied, place_ids[None, :], place_ids[None, :] + positions)
    place_of_slot = jnp.argsort(place_key, axis=1)[:, :LEAF_DEV].astype(jnp.int32)
    slot_used = jnp.arange(LEAF_DEV, dtype=jnp.int32)[None, :] < counts[:, None]
    return (slot_of.astype(jnp.int32), place_of_slot, slot_used)


def draw_neighbors(key, part):
    slot_of, place_of_slot, slot_used = leaf_layout(key)
    devices = SLOTS // LEAF_DEV
    cross_cells = CROSS_Y * CROSS_Z
    positions = PLANES * cross_cells
    device_ids = jnp.arange(devices, dtype=jnp.int32)[:, None]
    plane_x = device_ids * PLANES + place_of_slot // cross_cells
    coord_y = place_of_slot // CROSS_Z % CROSS_Y
    coord_z = place_of_slot % CROSS_Z
    flat_slots = slot_of.reshape(-1)
    columns = []
    for tap_number in range(27):
        if tap_number == 13:
            continue
        step_x = tap_number // 9 - 1
        step_y = tap_number // 3 % 3 - 1
        step_z = tap_number % 3 - 1
        near_x = plane_x + step_x
        near_y = coord_y + step_y
        near_z = coord_z + step_z
        inside = (near_x >= 0) & (near_x < devices * PLANES) & (near_y >= 0) & (near_y < CROSS_Y) & (near_z >= 0) & (near_z < CROSS_Z)
        near_device = jnp.clip(near_x, 0, devices * PLANES - 1) // PLANES
        near_place = jnp.clip(near_x, 0, devices * PLANES - 1) % PLANES * cross_cells + jnp.clip(near_y, 0, CROSS_Y - 1) * CROSS_Z + jnp.clip(near_z, 0, CROSS_Z - 1)
        lookup = jnp.clip(near_device * positions + near_place, 0, devices * positions - 1)
        near_slot = flat_slots[lookup]
        located = inside & slot_used & (near_slot >= 0)
        columns.append(jnp.where(located, near_device * LEAF_DEV + near_slot, -1))
    return jnp.stack(columns, axis=-1).reshape(SLOTS, 26).astype(jnp.int32)


def draw_mask_words(key, part):
    slot_of, place_of_slot, slot_used = leaf_layout(key)
    drawn = jax.random.randint(jax.random.fold_in(key, 29), (SLOTS, MASK_WORDS * 30), 0, 5)
    bit_values = (drawn < 3).astype(jnp.int32)
    within = (jnp.arange(MASK_WORDS * 30, dtype=jnp.int32) < VOXELS).astype(jnp.int32)
    bit_values = bit_values * within[None, :] * slot_used.reshape(SLOTS, 1).astype(jnp.int32)
    place_values = jnp.left_shift(jnp.ones((30,), jnp.int32), jnp.arange(30, dtype=jnp.int32))
    return jnp.sum(bit_values.reshape(SLOTS, MASK_WORDS, 30) * place_values[None, None, :], axis=2).astype(jnp.int32)


def shard_levels(rng, dims, cuts, low, high):
    def one(axis_at, parts):
        steps = jax.random.uniform(jax.random.fold_in(jax.random.fold_in(rng, 6), axis_at), (parts,), jnp.float32, low / len(cuts), high / len(cuts))
        return jnp.repeat(jnp.exp(steps), dims[axis_at] // parts).reshape((-1,) + (1,) * (len(dims) - axis_at - 1))

    factor_of = one(*cuts[0])
    for cut in cuts[1:]:
        factor_of = factor_of * one(*cut)
    return factor_of


def bell_draw(rng, dims, deviation, limit, pieces=(), kind=jnp.bfloat16):
    values = jax.random.normal(rng, dims, jnp.float32) * deviation
    if len(pieces) > 0:
        values = shard_levels(rng, dims, pieces, -0.22, 0.18) * values
    return jnp.clip(values, min=-limit, max=limit).astype(kind)


def setup_inputs(seed: int = 0, part: int = 0) -> dict:
    arg_keys = jax.random.split(jax.random.key(seed), 6)
    own_keys = jax.random.split(jax.random.fold_in(arg_keys[5], part), 6)
    features = bell_draw(own_keys[0], (SLOTS, C, VOXELS), 1.0, 6.0, ((0, 64),))
    cotangent = bell_draw(own_keys[1], (SLOTS, C, VOXELS), 1.0, 6.0, ((0, 64),))
    weight = bell_draw(arg_keys[2], (27, C, C), (27 * C) ** -0.5, 0.15625)
    mask_words = draw_mask_words(jax.random.fold_in(jax.random.fold_in(arg_keys[5], part), 71), part)
    neighbors = draw_neighbors(jax.random.fold_in(jax.random.fold_in(arg_keys[5], part), 71), part)
    return {"features": features, "cotangent": cotangent, "weight": weight, "mask_words": mask_words, "neighbors": neighbors}


def unpack_voxels(mask_words, voxel_count):
    bit_place = jnp.arange(30, dtype=jnp.int32)
    bit_values = jnp.right_shift(mask_words[:, :, None], bit_place[None, None, :]) & 1
    return bit_values.reshape(mask_words.shape[0], -1)[:, :voxel_count]


def edge_range(shift_value, extent):
    if shift_value < 0:
        return slice(extent - 1, extent)
    if shift_value > 0:
        return slice(0, 1)
    return slice(0, extent)


def tap_offsets():
    return [(shift_x, shift_y, shift_z) for shift_x in (-1, 0, 1) for shift_y in (-1, 0, 1) for shift_z in (-1, 0, 1)]


def assemble(center, fetch_piece):
    x_slabs = []
    for shift_x in (-1, 0, 1):
        y_rows = []
        for shift_y in (-1, 0, 1):
            z_cells = []
            for shift_z in (-1, 0, 1):
                if shift_x == 0 and shift_y == 0 and shift_z == 0:
                    z_cells.append(center)
                else:
                    z_cells.append(fetch_piece(shift_x, shift_y, shift_z))
            y_rows.append(jnp.concatenate(z_cells, axis=4))
        x_slabs.append(jnp.concatenate(y_rows, axis=3))
    return jnp.concatenate(x_slabs, axis=2)


def window(padded, offset, direction):
    extent = padded.shape[2] - 2
    start_x = 1 + direction * offset[0]
    start_y = 1 + direction * offset[1]
    start_z = 1 + direction * offset[2]
    piece = padded[:, :, start_x:start_x + extent, start_y:start_y + extent, start_z:start_z + extent]
    return piece.reshape(padded.shape[0], padded.shape[1], extent ** 3)


def reference(features, cotangent, weight, mask_words, neighbors):
    slot_total, channels, voxel_count = features.shape
    edge_cells = LEAF
    occupancy = unpack_voxels(mask_words, voxel_count).astype(jnp.bfloat16)
    masked_x = features * occupancy[:, None, :]
    masked_dy = cotangent * occupancy[:, None, :]
    shape_five = (slot_total, channels, edge_cells, edge_cells, edge_cells)
    block_x = masked_x.reshape(shape_five)
    block_dy = masked_dy.reshape(shape_five)
    offsets = tap_offsets()

    def sliced(block_field):
        table_list = []
        for offset in offsets:
            if offset == (0, 0, 0):
                table_list.append(None)
            else:
                table_list.append(block_field[:, :, edge_range(offset[0], edge_cells), edge_range(offset[1], edge_cells), edge_range(offset[2], edge_cells)])
        return table_list

    table_x = sliced(block_x)
    table_dy = sliced(block_dy)
    weight_wide = weight.astype(jnp.float32)
    group_size = LEAF_DEV
    block_count = slot_total // group_size

    def block_terms(inputs):
        near_block, center_x, center_dy, flat_dy = inputs

        def padded(center, table_list):
            def fetch_piece(shift_x, shift_y, shift_z):
                tap_number = (shift_x + 1) * 9 + (shift_y + 1) * 3 + shift_z + 1
                column = tap_number if tap_number < 13 else tap_number - 1
                row_index = near_block[:, column]
                picked = jnp.take(table_list[tap_number], jnp.clip(row_index, 0, slot_total - 1), axis=0)
                return jnp.where((row_index >= 0)[:, None, None, None, None], picked, jnp.zeros((), picked.dtype))
            return assemble(center, fetch_piece).astype(jnp.float32)

        pad_x = padded(center_x, table_x)
        pad_dy = padded(center_dy, table_dy)
        dy_wide = flat_dy.astype(jnp.float32)
        out_sum = jnp.zeros((group_size, channels, voxel_count), jnp.float32)
        back_sum = jnp.zeros((group_size, channels, voxel_count), jnp.float32)
        tap_grads = []
        for tap_number, offset in enumerate(offsets):
            ahead_cells = window(pad_x, offset, 1)
            behind_cells = window(pad_dy, offset, -1)
            out_sum = out_sum + jnp.einsum("io,liv->lov", weight_wide[tap_number], ahead_cells, precision=lax.Precision.HIGHEST)
            back_sum = back_sum + jnp.einsum("io,lov->liv", weight_wide[tap_number], behind_cells, precision=lax.Precision.HIGHEST)
            tap_grads.append(jnp.einsum("liv,lov->io", ahead_cells, dy_wide, precision=lax.Precision.HIGHEST))
        return out_sum, back_sum, jnp.stack(tap_grads)

    def regroup(array):
        return array.reshape((block_count, group_size) + array.shape[1:])

    out_parts, back_parts, grad_parts = lax.map(block_terms, (regroup(neighbors), regroup(block_x), regroup(block_dy), regroup(masked_dy)))
    occupancy_wide = occupancy.astype(jnp.float32)[:, None, :]
    out_features = (out_parts.reshape(slot_total, channels, voxel_count) * occupancy_wide).astype(jnp.bfloat16)
    in_grad = (back_parts.reshape(slot_total, channels, voxel_count) * occupancy_wide).astype(jnp.bfloat16)
    grad_scale = float(slot_total * voxel_count) ** -0.5
    weight_grad = jnp.sum(grad_parts, axis=0) * grad_scale
    return (out_features, in_grad, weight_grad)
```

```python
import functools

import jax
import jax.numpy as jnp
from jax import lax
from jax.experimental import pallas as pl
from jax.experimental.pallas import tpu as pltpu
from jax.sharding import PartitionSpec as P

LEAVES = 8
CH = 64
SIDE = 8
VOX = 512
PLANE = 64
ROWS = 80
NY = 4
TILES = 14
MESH = pl.DeviceIdType.MESH
F32 = jnp.float32
BF16 = jnp.bfloat16


def tap(p, q, r):
    return 9 * (p + 1) + 3 * (q + 1) + r + 1


def copy_to(src, dst, send, recv, dom):
    return pltpu.make_async_remote_copy(
        src_ref=src,
        dst_ref=dst,
        send_sem=send,
        recv_sem=recv,
        device_id={"dom": dom},
        device_id_type=MESH,
    )


def kernel(
    nz,
    scale,
    x_ref,
    dy_ref,
    w_ref,
    words_ref,
    near_ref,
    out_ref,
    back_ref,
    grad_ref,
    occ,
    xd,
    high,
    low,
    send_high,
    send_low,
    got_high,
    got_low,
    a0,
    a1,
    a2,
    zt,
    wf,
    wb,
    g,
    part,
    r1,
    u,
    r2,
    v,
    r3,
    own,
    f3,
    full,
    halo_sems,
    core_sems,
    y_sems,
    z_sems,
):
    ndom = nz * 8
    dom = lax.axis_index("dom")
    core = lax.rem(dom, 2)
    y = lax.rem(lax.div(dom, 2), NY)
    z = lax.div(dom, 8)
    up = lax.rem(dom + 1, ndom)
    down = lax.rem(dom + ndom - 1, ndom)
    mate = z * 8 + y * 2 + (1 - core)
    y_mates = [z * 8 + lax.rem(y + k, NY) * 2 + core for k in range(1, NY)]
    z_mates = [lax.rem(z + k, nz) * 8 + y * 2 + core for k in range(1, nz)]

    barrier = pltpu.get_barrier_semaphore()
    partners = [up, down, mate] + y_mates + z_mates
    for d in partners:
        pl.semaphore_signal(barrier, inc=1, device_id={"dom": d}, device_id_type=MESH)

    at = lax.broadcasted_iota(jnp.int32, (LEAVES, VOX), 1)
    word_at = lax.shift_right_logical(at * 2185, 16)
    bit_at = at - 30 * word_at
    words = jnp.zeros((LEAVES, VOX), jnp.int32)
    for n in range(18):
        words = jnp.where(word_at == n, words_ref[:, n : n + 1], words)
    bits = (lax.shift_right_logical(words, bit_at) & 1).astype(F32)
    for s in range(LEAVES):
        occ[s] = bits[s : s + 1]

    def prepare(s, carry):
        both = jnp.concatenate([x_ref[s].astype(F32), dy_ref[s].astype(F32)], axis=0)
        turned = (both * occ[s]).T.reshape(SIDE, SIDE, SIDE, 128)
        xd[s] = turned
        high[s] = turned[SIDE - 1]
        low[s] = turned[0]
        send_high[s] = turned[SIDE - 1].reshape(PLANE, 128).astype(BF16)
        send_low[s] = turned[0].reshape(PLANE, 128).astype(BF16)
        return carry

    lax.fori_loop(0, LEAVES, prepare, 0)
    xd[LEAVES] = jnp.zeros((SIDE, SIDE, SIDE, 128), F32)
    high[2 * LEAVES] = jnp.zeros((SIDE, SIDE, 128), F32)
    low[2 * LEAVES] = jnp.zeros((SIDE, SIDE, 128), F32)

    pl.semaphore_wait(barrier, len(partners))
    copy_up = copy_to(send_high, got_high, halo_sems.at[0, 0], halo_sems.at[0, 1], up)
    copy_down = copy_to(send_low, got_low, halo_sems.at[1, 0], halo_sems.at[1, 1], down)
    copy_up.start()
    copy_down.start()

    none = jnp.zeros((CH, CH), F32)

    def weight(p, q, r):
        return w_ref[tap(p, q, r)].astype(F32)

    for n, p in enumerate((-1, 0, 1)):
        rows = []
        for r in (-1, 0, 1):
            rows.append(
                jnp.concatenate([weight(p, -1, r), weight(p, 0, r), weight(p, 1, r), none], axis=1)
            )
        rows.append(jnp.zeros((CH, 4 * CH), F32))
        wf[n * 256 : (n + 1) * 256] = jnp.concatenate(rows, axis=0).astype(BF16)
        cols = []
        for q in (0, -1, None, 1):
            if q is None:
                cols.append(jnp.zeros((CH, 4 * CH), F32))
            else:
                cols.append(
                    jnp.concatenate(
                        [weight(-p, -q, 0), weight(-p, -q, 1), none, weight(-p, -q, -1)], axis=1
                    )
                )
        wb[n * 256 : (n + 1) * 256] = jnp.concatenate(cols, axis=0).T.astype(BF16)

    sub = lax.broadcasted_iota(jnp.int32, (10, SIDE, 128), 1)
    lane = lax.broadcasted_iota(jnp.int32, (10, SIDE, 128), 2)
    left = lane < CH
    first, last = sub == 0, sub == SIDE - 1

    def source(s, p, q, r):
        t = tap(p, q, r)
        if t == 13:
            return s
        n = near_ref[s, t if t < 13 else t - 1]
        slot = n & 7
        if p == 0:
            return jnp.where(n < 0, LEAVES, slot)
        here = lax.shift_right_arithmetic(n, 3) == dom
        return jnp.where(n < 0, 2 * LEAVES, jnp.where(here, slot, LEAVES + slot))

    def build(s, row, pool, ids):
        def line(r):
            return jnp.concatenate(
                [pool(ids[0, r], SIDE - 1, SIDE), pool(ids[1, r], 0, SIDE), pool(ids[2, r], 0, 1)],
                axis=0,
            )

        mid, before, after = line(1), line(0), line(2)
        less = pltpu.roll(jnp.where(last, before, mid), 1, 1)
        more = pltpu.roll(jnp.where(first, after, mid), SIDE - 1, 1)
        swapped = pltpu.roll(mid, CH, 2)
        a0[s, row] = jnp.where(left, less, swapped).reshape(ROWS, 128).astype(BF16)
        a1[s, row] = jnp.where(left, swapped, less).reshape(ROWS, 128).astype(BF16)
        a2[s, row] = more.reshape(ROWS, 128).astype(BF16)

    def inner(s, carry):
        ids = {(q + 1, r + 1): source(s, 0, q, r) for q in (-1, 0, 1) for r in (-1, 0, 1)}
        for a in range(SIDE):
            build(s, a + 1, lambda i, lo, hi, a=a: xd[i, a, lo:hi], ids)
        mine = xd[s]
        gap = jnp.zeros((SIDE, 1, SIDE, 128), F32)
        below = jnp.concatenate([mine, gap, gap], axis=1).reshape(SIDE * ROWS, 128)
        same = jnp.concatenate([gap, mine, gap], axis=1).reshape(SIDE * ROWS, 128)
        above = jnp.concatenate([gap, gap, mine], axis=1).reshape(SIDE * ROWS, 128)
        cols = pl.ds(pl.multiple_of(s * (SIDE * ROWS), 128), SIDE * ROWS)
        zt[0:CH, cols] = below.T[CH:].astype(BF16)
        zt[CH : 2 * CH, cols] = same.T[CH:].astype(BF16)
        zt[2 * CH :, cols] = above.T[CH:].astype(BF16)
        return carry

    lax.fori_loop(0, LEAVES, inner, 0)

    copy_up.wait()
    copy_down.wait()
    for s in range(LEAVES):
        high[LEAVES + s] = got_high[s].astype(F32).reshape(SIDE, SIDE, 128)
        low[LEAVES + s] = got_low[s].astype(F32).reshape(SIDE, SIDE, 128)

    def outer(s, carry):
        for p, row, pool in ((-1, 0, high), (1, SIDE + 1, low)):
            ids = {(q + 1, r + 1): source(s, p, q, r) for q in (-1, 0, 1) for r in (-1, 0, 1)}
            build(s, row, lambda i, lo, hi, pool=pool: pool[i, lo:hi], ids)
        return carry

    lax.fori_loop(0, LEAVES, outer, 0)

    for n in range(3):

        def term(h, total, n=n):
            cols = pl.ds(pl.multiple_of(h * (2 * SIDE * ROWS), 128), 2 * SIDE * ROWS)
            rows = pl.ds(h * 2, 2)
            right = jnp.concatenate(
                [
                    a0[rows, n : n + SIDE].reshape(2 * SIDE * ROWS, 128),
                    a2[rows, n : n + SIDE].reshape(2 * SIDE * ROWS, 128),
                ],
                axis=1,
            )
            return total + jnp.dot(zt[:, cols], right, preferred_element_type=F32)

        total = lax.fori_loop(0, LEAVES // 2, term, jnp.zeros((3 * CH, 256), F32))
        g[n] = total.T

    def put(index, value):
        part[index // TILES, index % TILES] = value

    for j in range(9):
        for k in range(8):
            at_row = (j % 3) * CH + 8 * k
            put(8 * j + k, g[j // 3, at_row : at_row + 8, 0:128])
    for j in range(5):
        lower = g[j // 3, (j % 3) * CH : (j % 3 + 1) * CH, 128:192]
        if j < 4:
            m = j + 5
            upper = g[m // 3, (m % 3) * CH : (m % 3 + 1) * CH, 128:192]
        else:
            upper = none
        pair = jnp.concatenate([lower, upper], axis=1)
        for k in range(8):
            put(72 + 8 * j + k, pair[8 * k : 8 * k + 8])

    half = lax.broadcasted_iota(jnp.int32, (SIDE * ROWS, 128), 1) < CH

    def convolve(s, carry):
        xs, ds = [], []
        for n in range(3):
            one = a0[s, n : n + SIDE].reshape(SIDE * ROWS, 128)
            two = a1[s, n : n + SIDE].reshape(SIDE * ROWS, 128)
            three = a2[s, n : n + SIDE].reshape(SIDE * ROWS, 128)
            xs += [one, three]
            ds += [two, three]
        yo = jnp.dot(jnp.concatenate(xs, axis=1), wf[...], preferred_element_type=F32)
        yb = jnp.dot(jnp.concatenate(ds, axis=1), wb[...], preferred_element_type=F32)
        shape = (SIDE, 10, SIDE, 128)
        ahead = (yo[:, 128:] + yb[:, 128:]).reshape(shape)
        behind = jnp.where(half, yo[:, :128], yb[:, :128]).reshape(shape)
        level = pltpu.roll(jnp.where(half, yb[:, :128], yo[:, :128]), CH, 1).reshape(shape)
        total = behind[:, 0:8] + level[:, 1:9] + ahead[:, 2:10]
        turned = total.reshape(VOX, 128).T * occ[s]
        out_ref[s] = turned[:CH].astype(BF16)
        back_ref[s] = turned[CH:].astype(BF16)
        return carry

    theirs, ours = pl.ds((1 - core) * NY, NY), pl.ds(core * NY, NY)
    c1 = copy_to(part.at[theirs], r1, core_sems.at[0, 0], core_sems.at[0, 1], mate)
    c1.start()
    lax.fori_loop(0, 1, convolve, 0)
    c1.wait()
    for k in range(NY):
        u[k] = part[core * NY + k] + r1[k]
    c2 = [
        copy_to(
            u.at[lax.rem(y + k, NY)], r2.at[k - 1], y_sems.at[0, k - 1], y_sems.at[1, k - 1], y_mates[k - 1]
        )
        for k in range(1, NY)
    ]
    for c in c2:
        c.start()
    lax.fori_loop(1, 3, convolve, 0)
    for c in c2:
        c.wait()
    v[0:TILES] = u[y] + r2[0] + r2[1] + r2[2]
    v[TILES:] = jnp.zeros((16 - TILES, 8, 128), F32)
    per = 16 // nz
    c3 = [
        copy_to(
            v.at[pl.ds(lax.rem(z + k, nz) * per, per)],
            r3.at[k - 1],
            z_sems.at[0, k - 1],
            z_sems.at[1, k - 1],
            z_mates[k - 1],
        )
        for k in range(1, nz)
    ]
    for c in c3:
        c.start()
    lax.fori_loop(3, 4, convolve, 0)
    for c in c3:
        c.wait()
    mine = v[pl.ds(z * per, per)]
    for k in range(nz - 1):
        mine = mine + r3[k]
    own[...] = mine * scale
    c4 = [
        copy_to(
            own, f3.at[pl.ds(z * per, per)], z_sems.at[2, k - 1], z_sems.at[3, k - 1], z_mates[k - 1]
        )
        for k in range(1, nz)
    ]
    for c in c4:
        c.start()
    f3[pl.ds(z * per, per)] = own[...]
    lax.fori_loop(4, 5, convolve, 0)
    for c in c4:
        c.wait()
    c5 = [
        copy_to(
            f3.at[pl.ds(0, TILES)],
            full.at[core * NY + y],
            y_sems.at[2, k - 1],
            y_sems.at[3, k - 1],
            y_mates[k - 1],
        )
        for k in range(1, NY)
    ]
    for c in c5:
        c.start()
    full[core * NY + y] = f3[0:TILES]
    lax.fori_loop(5, 7, convolve, 0)
    for c in c5:
        c.wait()
    c6 = copy_to(full.at[ours], full.at[ours], core_sems.at[1, 0], core_sems.at[1, 1], mate)
    c6.start()
    lax.fori_loop(7, 8, convolve, 0)
    c6.wait()

    def tile(index):
        return full[index // TILES, index % TILES]

    for j in range(9):
        p, r = j // 3 - 1, j % 3 - 1
        for k in range(8):
            rows = slice(8 * k, 8 * k + 8)
            value = tile(8 * j + k)
            grad_ref[tap(p, -1, r), rows] = value[:, :CH]
            grad_ref[tap(p, 0, r), rows] = value[:, CH:]
            m = j if j < 5 else j - 5
            value = tile(72 + 8 * m + k)
            grad_ref[tap(p, 1, r), rows] = value[:, :CH] if j < 5 else value[:, CH:]


def shards(nz, features, cotangent, weight, mask_words, neighbors):
    scale = float(nz * 8 * LEAVES * VOX) ** -0.5
    vmem = pltpu.VMEM
    per = 16 // nz
    dma = pltpu.SemaphoreType.DMA
    any_vmem = pl.BlockSpec(memory_space=pltpu.VMEM)
    field = jax.ShapeDtypeStruct((LEAVES, CH, VOX), BF16)
    return pl.pallas_call(
        functools.partial(kernel, nz, scale),
        out_shape=(field, field, jax.ShapeDtypeStruct((27, CH, CH), F32)),
        in_specs=[any_vmem] * 4 + [pl.BlockSpec(memory_space=pltpu.SMEM)],
        out_specs=(any_vmem,) * 3,
        scratch_shapes=[
            vmem((LEAVES, 1, VOX), F32),
            vmem((LEAVES + 1, SIDE, SIDE, SIDE, 128), F32),
            vmem((2 * LEAVES + 1, SIDE, SIDE, 128), F32),
            vmem((2 * LEAVES + 1, SIDE, SIDE, 128), F32),
            vmem((LEAVES, PLANE, 128), BF16),
            vmem((LEAVES, PLANE, 128), BF16),
            vmem((LEAVES, PLANE, 128), BF16),
            vmem((LEAVES, PLANE, 128), BF16),
            vmem((LEAVES, 10, ROWS, 128), BF16),
            vmem((LEAVES, 10, ROWS, 128), BF16),
            vmem((LEAVES, 10, ROWS, 128), BF16),
            vmem((3 * CH, LEAVES * SIDE * ROWS), BF16),
            vmem((768, 256), BF16),
            vmem((768, 256), BF16),
            vmem((3, 256, 192), F32),
            vmem((8, TILES, 8, 128), F32),
            vmem((NY, TILES, 8, 128), F32),
            vmem((NY, TILES, 8, 128), F32),
            vmem((NY - 1, TILES, 8, 128), F32),
            vmem((16, 8, 128), F32),
            vmem((nz - 1, per, 8, 128), F32),
            vmem((per, 8, 128), F32),
            vmem((16, 8, 128), F32),
            vmem((8, TILES, 8, 128), F32),
            dma((2, 2)),
            dma((2, 2)),
            dma((4, NY - 1)),
            dma((4, nz - 1)),
        ],
        compiler_params=pltpu.CompilerParams(
            collective_id=0, has_side_effects=True, vmem_limit_bytes=48 * 2**20
        ),
        name="sparse_conv",
    )(features, cotangent, weight, mask_words, neighbors)


def solution(mesh):
    placed = (
        P(("scene", "dom"), None, None),
        P(("scene", "dom"), None, None),
        P(),
        P(("scene", "dom"), None),
        P(("scene", "dom"), None),
    )
    return jax.shard_map(
        functools.partial(shards, mesh.shape["dom"] // 8),
        mesh=mesh,
        in_specs=placed,
        out_specs=(
            P(("scene", "dom"), None, None),
            P(("scene", "dom"), None, None),
            P("scene", None, None),
        ),
        check_vma=False,
    )
```

```python
import functools

import jax
import jax.numpy as jnp
from jax import lax
from jax.experimental import pallas as pl
from jax.experimental.pallas import tpu as pltpu
from jax.sharding import PartitionSpec as P

LEAVES = 8
CH = 64
SIDE = 8
VOX = 512
PLANE = 64
ROWS = 80
WIDE = 640
MESH = pl.DeviceIdType.MESH
F32 = jnp.float32
BF16 = jnp.bfloat16


def tap(p, q, r):
    return 9 * (p + 1) + 3 * (q + 1) + r + 1


def copy_to(src, dst, send, recv, dom):
    return pltpu.make_async_remote_copy(
        src_ref=src,
        dst_ref=dst,
        send_sem=send,
        recv_sem=recv,
        device_id={"dom": dom},
        device_id_type=MESH,
    )


def kernel(
    cells,
    scale,
    x_hbm,
    dy_hbm,
    w_hbm,
    words_hbm,
    near_hbm,
    out_hbm,
    back_hbm,
    grad_hbm,
    out_ref,
    back_ref,
    grad_ref,
    x_ref,
    dy_ref,
    w_ref,
    words_ref,
    near_ref,
    occ,
    xd,
    high,
    low,
    send_high,
    send_low,
    got_high,
    got_low,
    a0,
    a1,
    a2,
    zt,
    wf,
    wb,
    g,
    sums,
    part,
    mates,
    summed,
    terms,
    own,
    full,
    in_sems,
    out_sems,
    halo_sems,
    core_sems,
    scatter_sent,
    scatter_got,
    gather_sent,
    gather_got,
):
    ndom = cells * 2
    dom = lax.axis_index("dom")
    core = lax.rem(dom, 2)
    cell = lax.div(dom, 2)
    up = lax.rem(dom + 1, ndom)
    down = lax.rem(dom + ndom - 1, ndom)
    mate = dom + 1 - 2 * core
    groups, per = part.shape[2:4]
    middle = cells // 2 + 2

    fetches = [
        pltpu.make_async_copy(source, dest, in_sems.at[n])
        for n, (source, dest) in enumerate(
            (
                (words_hbm, words_ref),
                (x_hbm, x_ref),
                (dy_hbm, dy_ref),
                (near_hbm, near_ref),
                (w_hbm, w_ref),
            )
        )
    ]
    for fetch in fetches:
        fetch.start()

    barrier = pltpu.get_barrier_semaphore()

    def greet(k, carry):
        to = lax.rem(cell + k, cells) * 2 + core
        pl.semaphore_signal(barrier, inc=1, device_id={"dom": to}, device_id_type=MESH)
        return carry

    for d in (up, down, mate):
        pl.semaphore_signal(barrier, inc=1, device_id={"dom": d}, device_id_type=MESH)
    lax.fori_loop(1, cells, greet, 0)
    fetches[0].wait()

    at = lax.broadcasted_iota(jnp.int32, (LEAVES, VOX), 1)
    word_at = lax.shift_right_logical(at * 2185, 16)
    bit_at = at - 30 * word_at
    words = jnp.zeros((LEAVES, VOX), jnp.int32)
    for n in range(18):
        words = jnp.where(word_at == n, words_ref[:, n : n + 1], words)
    bits = (lax.shift_right_logical(words, bit_at) & 1).astype(F32)
    for s in range(LEAVES):
        occ[s] = bits[s : s + 1]

    def prepare(s, carry):
        both = jnp.concatenate([x_ref[s].astype(F32), dy_ref[s].astype(F32)], axis=0)
        turned = (both * occ[s]).T.reshape(SIDE, SIDE, SIDE, 128)
        xd[s] = turned
        high[s] = turned[SIDE - 1]
        low[s] = turned[0]
        send_high[s] = turned[SIDE - 1].reshape(PLANE, 128).astype(BF16)
        send_low[s] = turned[0].reshape(PLANE, 128).astype(BF16)
        return carry

    fetches[1].wait()
    fetches[2].wait()
    lax.fori_loop(0, LEAVES, prepare, 0)
    xd[LEAVES] = jnp.zeros((SIDE, SIDE, SIDE, 128), F32)
    high[2 * LEAVES] = jnp.zeros((SIDE, SIDE, 128), F32)
    low[2 * LEAVES] = jnp.zeros((SIDE, SIDE, 128), F32)

    pl.semaphore_wait(barrier, cells + 2)
    copy_up = copy_to(send_high, got_high, halo_sems.at[0, 0], halo_sems.at[0, 1], up)
    copy_down = copy_to(send_low, got_low, halo_sems.at[1, 0], halo_sems.at[1, 1], down)
    copy_up.start()
    copy_down.start()

    none = jnp.zeros((CH, CH), F32)
    sub = lax.broadcasted_iota(jnp.int32, (10, SIDE, 128), 1)
    lane = lax.broadcasted_iota(jnp.int32, (10, SIDE, 128), 2)
    left = lane < CH
    first, last = sub == 0, sub == SIDE - 1

    def source(s, p, q, r):
        t = tap(p, q, r)
        if t == 13:
            return s
        n = near_ref[s, t if t < 13 else t - 1]
        slot = n & 7
        if p == 0:
            return jnp.where(n < 0, LEAVES, slot)
        here = lax.shift_right_arithmetic(n, 3) == dom
        return jnp.where(n < 0, 2 * LEAVES, jnp.where(here, slot, LEAVES + slot))

    def build(s, row, pool, ids):
        def line(r):
            return jnp.concatenate(
                [pool(ids[0, r], SIDE - 1, SIDE), pool(ids[1, r], 0, SIDE), pool(ids[2, r], 0, 1)],
                axis=0,
            )

        mid, before, after = line(1), line(0), line(2)
        less = pltpu.roll(jnp.where(last, before, mid), 1, 1)
        more = pltpu.roll(jnp.where(first, after, mid), SIDE - 1, 1)
        swapped = pltpu.roll(mid, CH, 2)
        a0[row, s] = jnp.where(left, less, swapped).reshape(ROWS, 128).astype(BF16)
        a1[row, s] = jnp.where(left, swapped, less).reshape(ROWS, 128).astype(BF16)
        a2[row, s] = more.reshape(ROWS, 128).astype(BF16)

    def inner(s, carry):
        ids = {(q + 1, r + 1): source(s, 0, q, r) for q in (-1, 0, 1) for r in (-1, 0, 1)}
        for a in range(SIDE):
            build(s, a + 1, lambda i, lo, hi, a=a: xd[i, a, lo:hi], ids)
        return carry

    gap = jnp.zeros((LEAVES, 1, SIDE, 128), F32)

    def spread(field, q):
        parts = [gap, gap]
        parts.insert(q + 1, field)
        return jnp.concatenate(parts, axis=1).reshape(WIDE, 128)

    def turn(h, carry):
        a, b = 2 * h, 2 * h + 1
        one, two = xd[0:LEAVES, a], xd[0:LEAVES, b]
        cols = [pl.ds(pl.multiple_of(plane * WIDE, 128), WIDE) for plane in (a, b)]
        side = lax.broadcasted_iota(jnp.int32, (WIDE, 128), 1) < CH
        rolled = [pltpu.roll(one, CH, 3), pltpu.roll(two, CH, 3)]
        for n, field in enumerate((one, two)):
            both = jnp.where(side, spread(rolled[n], -1), spread(field, 0))
            zt[0 : 2 * CH, cols[n]] = both.astype(BF16).T
        both = jnp.where(side, spread(rolled[0], 1), spread(two, 1)).astype(BF16).T
        zt[2 * CH :, cols[0]] = both[:CH]
        zt[2 * CH :, cols[1]] = both[CH:]
        return carry

    def planes(p, a, count):
        right = jnp.concatenate(
            [
                a0[pl.ds(a + p + 1, count)].reshape(count * WIDE, 128),
                a2[pl.ds(a + p + 1, count)].reshape(count * WIDE, 128),
            ],
            axis=1,
        )
        cols = pl.ds(pl.multiple_of(a * WIDE, 128), count * WIDE)
        return jnp.dot(zt[:, cols], right, preferred_element_type=F32)

    def gradient(n, p, start, pairs):
        total = lax.fori_loop(
            0,
            pairs,
            lambda h, t: t + planes(p, start + 2 * h, 2),
            jnp.zeros((3 * CH, 256), F32),
        )
        if pairs < 4:
            total = total + planes(p, start + 2 * pairs, 1)
        sums[n] = total

    def lay(n):
        g[...] = sums[n].T

        def put(t, value):
            part[n, t // 18, t % 18 // per, t % 18 % per] = value

        for t in range(24):
            put(t, g[8 * t : 8 * t + 8, 0:128])
        ahead = jnp.concatenate([g[0:CH, 128:], g[CH : 2 * CH, 128:]], axis=1)
        for t in range(8):
            put(24 + t, ahead[8 * t : 8 * t + 8])
        ahead = jnp.concatenate([g[2 * CH : 160, 128:], g[160:192, 128:]], axis=1)
        for t in range(4):
            put(32 + t, ahead[8 * t : 8 * t + 8])

    def give(n, p):
        for t in range(36):
            value = full[n, t // 18, t % 18 // per, t % 18 % per]
            if t < 24:
                r, rows = t // 8 - 1, slice(t % 8 * 8, t % 8 * 8 + 8)
                grad_ref[tap(p, -1, r), rows] = value[:, :CH]
                grad_ref[tap(p, 0, r), rows] = value[:, CH:]
            elif t < 32:
                rows = slice((t - 24) * 8, (t - 24) * 8 + 8)
                grad_ref[tap(p, 1, -1), rows] = value[:, :CH]
                grad_ref[tap(p, 1, 0), rows] = value[:, CH:]
            else:
                at_row = (t - 32) * 8
                grad_ref[tap(p, 1, 1), at_row : at_row + 8] = value[:, :CH]
                grad_ref[tap(p, 1, 1), 32 + at_row : 40 + at_row] = value[:, CH:]

    def pair(n):
        return copy_to(part.at[n, 1 - core], mates.at[n], core_sems.at[0, n], core_sems.at[1, n], mate)

    def pair_back(n):
        whole = full.at[n, core]
        return copy_to(whole, whole, core_sems.at[2, n], core_sems.at[3, n], mate)

    def scatter(n, to, j):
        k = lax.rem(to - cell + cells, cells)
        return copy_to(
            summed.at[n, j], terms.at[n, k], scatter_sent.at[n], scatter_got.at[n], to * 2 + core
        )

    def gather(n, k, j):
        to = lax.rem(cell + k, cells)
        return copy_to(
            own.at[n], full.at[n, core, j], gather_sent.at[n], gather_got.at[n], to * 2 + core
        )

    def whole(ref, sent, got):
        return copy_to(ref, ref, sent, got, mate)

    def owning(n, do):
        j = mine(n)

        @pl.when(j < groups)
        def _():
            do(True, j)

        @pl.when(j >= groups)
        def _():
            do(False, j)

    def scatter_sent_wait(n):
        def do(owns, j):
            ref = summed.at[n, pl.ds(0, groups - owns)]
            whole(ref, scatter_sent.at[n], scatter_got.at[n]).wait_send()

        owning(n, do)

    def gather_got_wait(n):
        def do(owns, j):
            ref = full.at[n, core, pl.ds(0, groups - owns)]
            whole(ref, gather_sent.at[n], gather_got.at[n]).wait_recv()

        owning(n, do)

    def gather_sent_wait(n):
        @pl.when(mine(n) < groups)
        def _():
            ref = terms.at[n, pl.ds(1, cells - 1)]
            whole(ref, gather_sent.at[n], gather_got.at[n]).wait_send()

    def far_first(do):
        def step(k, carry):
            do(k)
            return carry

        lax.fori_loop(1, cells, step, 0)

    def mine(n):
        return lax.rem(cell - groups * n + 4 * cells, cells)

    def scatter_start(n):
        pair(n).wait()
        summed[n] = part[n, core] + mates[n]

        def send(k):
            to = lax.rem(cell + k, cells)
            j = lax.rem(to - groups * n + 4 * cells, cells)

            @pl.when(j < groups)
            def _():
                scatter(n, to, j).start()

        far_first(send)

    def gather_start(n):
        j = mine(n)

        @pl.when(j < groups)
        def _():
            total = summed[n, j]
            whole(terms.at[n, pl.ds(1, cells - 1)], scatter_sent.at[n], scatter_got.at[n]).wait_recv()
            for k in range(1, cells):
                total = total + terms[n, k]
            own[n] = total * scale
            far_first(lambda k: gather(n, k, j).start())
            full[n, core, j] = own[n]

    def pair_back_start(n):
        gather_got_wait(n)
        pair_back(n).start()

    def finish(n, p):
        pair_back(n).wait()
        give(n, p)

    fetches[3].wait()
    lax.fori_loop(0, LEAVES, inner, 0)
    lax.fori_loop(0, SIDE // 2, turn, 0)
    gradient(0, 0, 0, 4)
    lay(0)
    pair(0).start()
    gradient(1, -1, 1, 3)
    gradient(2, 1, 0, 3)
    scatter_start(0)
    copy_up.wait()
    copy_down.wait()
    for s in range(LEAVES):
        high[LEAVES + s] = got_high[s].astype(F32).reshape(SIDE, SIDE, 128)
        low[LEAVES + s] = got_low[s].astype(F32).reshape(SIDE, SIDE, 128)

    def outer(s, carry):
        for p, row, pool in ((-1, 0, high), (1, SIDE + 1, low)):
            ids = {(q + 1, r + 1): source(s, p, q, r) for q in (-1, 0, 1) for r in (-1, 0, 1)}
            build(s, row, lambda i, lo, hi, pool=pool: pool[i, lo:hi], ids)
        return carry

    lax.fori_loop(0, LEAVES, outer, 0)

    half = lax.broadcasted_iota(jnp.int32, (WIDE, 128), 1) < CH

    def convolve(s, carry):
        xs, ds = [], []
        for n in range(3):
            one = a0[n : n + SIDE, s].reshape(WIDE, 128)
            two = a1[n : n + SIDE, s].reshape(WIDE, 128)
            three = a2[n : n + SIDE, s].reshape(WIDE, 128)
            xs += [one, three]
            ds += [two, three]
        yo = jnp.dot(jnp.concatenate(xs, axis=1), wf[...], preferred_element_type=F32)
        yb = jnp.dot(jnp.concatenate(ds, axis=1), wb[...], preferred_element_type=F32)
        shape = (SIDE, 10, SIDE, 128)
        ahead = (yo[:, 128:] + yb[:, 128:]).reshape(shape)
        behind = jnp.where(half, yo[:, :128], yb[:, :128]).reshape(shape)
        level = pltpu.roll(jnp.where(half, yb[:, :128], yo[:, :128]), CH, 1).reshape(shape)
        total = behind[:, 0:8] + level[:, 1:9] + ahead[:, 2:10]
        turned = total.reshape(VOX, 128).T * occ[s]
        out_ref[s] = turned[:CH].astype(BF16)
        back_ref[s] = turned[CH:].astype(BF16)
        return carry

    sums[1] += planes(-1, 0, 1)
    lay(1)
    pair(1).start()
    sums[2] += planes(1, SIDE - 1, 1)
    lay(2)
    pair(2).start()

    fetches[4].wait()

    def weight(p, q, r):
        return w_ref[tap(p, q, r)].astype(F32)

    for n, p in enumerate((-1, 0, 1)):
        rows = []
        for r in (-1, 0, 1):
            rows.append(
                jnp.concatenate([weight(p, -1, r), weight(p, 0, r), weight(p, 1, r), none], axis=1)
            )
        rows.append(jnp.zeros((CH, 4 * CH), F32))
        wf[n * 256 : (n + 1) * 256] = jnp.concatenate(rows, axis=0).astype(BF16)
        cols = []
        for q in (0, -1, None, 1):
            if q is None:
                cols.append(jnp.zeros((CH, 4 * CH), F32))
            else:
                cols.append(
                    jnp.concatenate(
                        [weight(-p, -q, 0), weight(-p, -q, 1), none, weight(-p, -q, -1)], axis=1
                    )
                )
        wb[n * 256 : (n + 1) * 256] = jnp.concatenate(cols, axis=0).T.astype(BF16)

    scatter_start(1)
    scatter_start(2)
    gather_start(0)
    lax.fori_loop(0, 6, convolve, 0)
    gather_start(1)
    gather_start(2)
    lax.fori_loop(6, 8, convolve, 0)
    leave = [
        pltpu.make_async_copy(out_ref, out_hbm, out_sems.at[0]),
        pltpu.make_async_copy(back_ref, back_hbm, out_sems.at[1]),
    ]
    leave[0].start()
    leave[1].start()

    def grad_leave(n, p):
        rows = pl.ds(9 * (p + 1), 9)
        leave.append(
            pltpu.make_async_copy(grad_ref.at[rows], grad_hbm.at[rows], out_sems.at[2 + n])
        )
        leave[-1].start()

    for n in range(3):
        scatter_sent_wait(n)
    pair_back_start(0)
    finish(0, 0)
    grad_leave(0, 0)
    pair_back_start(1)
    pair_back_start(2)
    for n in range(3):
        gather_sent_wait(n)
    finish(1, -1)
    grad_leave(1, -1)
    finish(2, 1)
    grad_leave(2, 1)
    for copy in leave:
        copy.wait()


PIECES = ((0, 0, 4), (0, 4, 4), (1, 0, 4), (1, 4, 4), (2, 0, 9), (2, 9, 9), (2, 18, 9))


def write_out(*refs):
    sems = refs[9]
    ins, outs = [], []
    for n, (which, start, count) in enumerate(PIECES):
        rows = pl.ds(start, count)
        source, dest, held = (refs[which + m].at[rows] for m in (0, 3, 6))
        ins.append(pltpu.make_async_copy(source, held, sems.at[0, n]))
        outs.append(pltpu.make_async_copy(held, dest, sems.at[1, n]))
    for copy in ins:
        copy.start()
    for n, copy in enumerate(ins):
        copy.wait()
        outs[n].start()
    for copy in outs:
        copy.wait()


def shards(cells, features, cotangent, weight, mask_words, neighbors):
    scale = float(cells * 2 * LEAVES * VOX) ** -0.5
    vmem = pltpu.VMEM
    dma = pltpu.SemaphoreType.DMA
    in_hbm = pl.BlockSpec(memory_space=pltpu.HBM)
    field = jax.ShapeDtypeStruct((LEAVES, CH, VOX), BF16)
    results = (field, field, jax.ShapeDtypeStruct((27, CH, CH), F32))
    per = -(-18 // cells)
    groups = 18 // per
    tiles = (groups, per, 8, 128)
    made = pl.pallas_call(
        functools.partial(kernel, cells, scale),
        out_shape=results,
        in_specs=[in_hbm] * 5,
        out_specs=(in_hbm,) * 3,
        scratch_shapes=[
            vmem((LEAVES, CH, VOX), BF16),
            vmem((LEAVES, CH, VOX), BF16),
            vmem((27, CH, CH), F32),
            vmem((LEAVES, CH, VOX), BF16),
            vmem((LEAVES, CH, VOX), BF16),
            vmem((27, CH, CH), BF16),
            vmem(mask_words.shape, jnp.int32),
            pltpu.SMEM(neighbors.shape, jnp.int32),
            vmem((LEAVES, 1, VOX), F32),
            vmem((LEAVES + 1, SIDE, SIDE, SIDE, 128), F32),
            vmem((2 * LEAVES + 1, SIDE, SIDE, 128), F32),
            vmem((2 * LEAVES + 1, SIDE, SIDE, 128), F32),
            vmem((LEAVES, PLANE, 128), BF16),
            vmem((LEAVES, PLANE, 128), BF16),
            vmem((LEAVES, PLANE, 128), BF16),
            vmem((LEAVES, PLANE, 128), BF16),
            vmem((10, LEAVES, ROWS, 128), BF16),
            vmem((10, LEAVES, ROWS, 128), BF16),
            vmem((10, LEAVES, ROWS, 128), BF16),
            vmem((3 * CH, LEAVES * WIDE), BF16),
            vmem((768, 256), BF16),
            vmem((768, 256), BF16),
            vmem((256, 192), F32),
            vmem((3, 192, 256), F32),
            vmem((3, 2) + tiles, F32),
            vmem((3,) + tiles, F32),
            vmem((3,) + tiles, F32),
            vmem((3, cells) + tiles[1:], F32),
            vmem((3,) + tiles[1:], F32),
            vmem((3, 2) + tiles, F32),
            dma((5,)),
            dma((5,)),
            dma((2, 2)),
            dma((4, 3)),
            dma((3,)),
            dma((3,)),
            dma((3,)),
            dma((3,)),
        ],
        compiler_params=pltpu.CompilerParams(
            collective_id=0, has_side_effects=True, vmem_limit_bytes=60_000_000
        ),
        name="sparse_conv",
    )(features, cotangent, weight, mask_words, neighbors)
    return pl.pallas_call(
        write_out,
        out_shape=results,
        in_specs=[in_hbm] * 3,
        out_specs=(in_hbm,) * 3,
        scratch_shapes=[vmem(r.shape, r.dtype) for r in results] + [dma((2, len(PIECES)))],
        compiler_params=pltpu.CompilerParams(vmem_limit_bytes=60_000_000),
        name="write_out",
    )(*made)


def solution(mesh):
    placed = (
        P(("scene", "dom"), None, None),
        P(("scene", "dom"), None, None),
        P(),
        P(("scene", "dom"), None),
        P(("scene", "dom"), None),
    )
    return jax.shard_map(
        functools.partial(shards, mesh.shape["dom"] // 2),
        mesh=mesh,
        in_specs=placed,
        out_specs=(
            P(("scene", "dom"), None, None),
            P(("scene", "dom"), None, None),
            P("scene", None, None),
        ),
        check_vma=False,
    )
```

```python
import functools

import jax
import jax.numpy as jnp
from jax import lax
from jax.experimental import pallas as pl
from jax.experimental.pallas import tpu as pltpu
from jax.sharding import PartitionSpec as P

LEAVES = 8
CH = 64
SIDE = 8
VOX = 512
PLANE = 64
ROWS = 80
WIDE = 640
MESH = pl.DeviceIdType.MESH
F32 = jnp.float32
BF16 = jnp.bfloat16


def tap(p, q, r):
    return 9 * (p + 1) + 3 * (q + 1) + r + 1


def copy_to(src, dst, send, recv, dom):
    return pltpu.make_async_remote_copy(
        src_ref=src,
        dst_ref=dst,
        send_sem=send,
        recv_sem=recv,
        device_id={"dom": dom},
        device_id_type=MESH,
    )


def kernel(
    cells,
    scale,
    x_hbm,
    dy_hbm,
    w_hbm,
    words_hbm,
    near_hbm,
    out_hbm,
    back_hbm,
    grad_hbm,
    out_ref,
    back_ref,
    grad_ref,
    x_ref,
    dy_ref,
    w_ref,
    words_ref,
    near_ref,
    occ,
    xd,
    high,
    low,
    send_high,
    send_low,
    got_high,
    got_low,
    a0,
    a1,
    a2,
    zt,
    wf,
    wb,
    g,
    sums,
    part,
    mates,
    summed,
    terms,
    own,
    full,
    in_sems,
    out_sems,
    halo_sems,
    core_sems,
    scatter_sent,
    scatter_got,
    gather_sent,
    gather_got,
):
    ndom = cells * 2
    dom = lax.axis_index("dom")
    core = lax.rem(dom, 2)
    cell = lax.div(dom, 2)
    up = lax.rem(dom + 1, ndom)
    down = lax.rem(dom + ndom - 1, ndom)
    mate = dom + 1 - 2 * core
    groups, per = part.shape[2:4]
    middle = cells // 2 + 2

    fetches = [
        pltpu.make_async_copy(source, dest, in_sems.at[n])
        for n, (source, dest) in enumerate(
            (
                (words_hbm, words_ref),
                (x_hbm, x_ref),
                (dy_hbm, dy_ref),
                (near_hbm, near_ref),
                (w_hbm, w_ref),
            )
        )
    ]
    for fetch in fetches:
        fetch.start()

    barrier = pltpu.get_barrier_semaphore()

    def greet(k, carry):
        to = lax.rem(cell + k, cells) * 2 + core
        pl.semaphore_signal(barrier, inc=1, device_id={"dom": to}, device_id_type=MESH)
        return carry

    for d in (up, down, mate):
        pl.semaphore_signal(barrier, inc=1, device_id={"dom": d}, device_id_type=MESH)
    lax.fori_loop(1, cells, greet, 0)
    fetches[0].wait()

    at = lax.broadcasted_iota(jnp.int32, (LEAVES, VOX), 1)
    word_at = lax.shift_right_logical(at * 2185, 16)
    bit_at = at - 30 * word_at
    words = jnp.zeros((LEAVES, VOX), jnp.int32)
    for n in range(18):
        words = jnp.where(word_at == n, words_ref[:, n : n + 1], words)
    bits = (lax.shift_right_logical(words, bit_at) & 1).astype(F32)
    for s in range(LEAVES):
        occ[s] = bits[s : s + 1]

    def prepare(s, carry):
        both = jnp.concatenate([x_ref[s].astype(F32), dy_ref[s].astype(F32)], axis=0)
        turned = (both * occ[s]).T.reshape(SIDE, SIDE, SIDE, 128)
        xd[s] = turned
        high[s] = turned[SIDE - 1]
        low[s] = turned[0]
        send_high[s] = turned[SIDE - 1].reshape(PLANE, 128).astype(BF16)
        send_low[s] = turned[0].reshape(PLANE, 128).astype(BF16)
        return carry

    fetches[1].wait()
    fetches[2].wait()
    lax.fori_loop(0, LEAVES, prepare, 0)
    xd[LEAVES] = jnp.zeros((SIDE, SIDE, SIDE, 128), F32)
    high[2 * LEAVES] = jnp.zeros((SIDE, SIDE, 128), F32)
    low[2 * LEAVES] = jnp.zeros((SIDE, SIDE, 128), F32)


    none = jnp.zeros((CH, CH), F32)
    sub = lax.broadcasted_iota(jnp.int32, (10, SIDE, 128), 1)
    lane = lax.broadcasted_iota(jnp.int32, (10, SIDE, 128), 2)
    left = lane < CH
    first, last = sub == 0, sub == SIDE - 1

    def source(s, p, q, r):
        t = tap(p, q, r)
        if t == 13:
            return s
        n = near_ref[s, t if t < 13 else t - 1]
        slot = n & 7
        if p == 0:
            return jnp.where(n < 0, LEAVES, slot)
        here = lax.shift_right_arithmetic(n, 3) == dom
        return jnp.where(n < 0, 2 * LEAVES, jnp.where(here, slot, LEAVES + slot))

    def build(s, row, pool, ids):
        def line(r):
            return jnp.concatenate(
                [pool(ids[0, r], SIDE - 1, SIDE), pool(ids[1, r], 0, SIDE), pool(ids[2, r], 0, 1)],
                axis=0,
            )

        mid, before, after = line(1), line(0), line(2)
        less = pltpu.roll(jnp.where(last, before, mid), 1, 1)
        more = pltpu.roll(jnp.where(first, after, mid), SIDE - 1, 1)
        swapped = pltpu.roll(mid, CH, 2)
        a0[row, s] = jnp.where(left, less, swapped).reshape(ROWS, 128).astype(BF16)
        a1[row, s] = jnp.where(left, swapped, less).reshape(ROWS, 128).astype(BF16)
        a2[row, s] = more.reshape(ROWS, 128).astype(BF16)

    def inner(s, carry):
        ids = {(q + 1, r + 1): source(s, 0, q, r) for q in (-1, 0, 1) for r in (-1, 0, 1)}
        for a in range(SIDE):
            build(s, a + 1, lambda i, lo, hi, a=a: xd[i, a, lo:hi], ids)
        return carry

    gap = jnp.zeros((LEAVES, 1, SIDE, 128), F32)

    def spread(field, q):
        parts = [gap, gap]
        parts.insert(q + 1, field)
        return jnp.concatenate(parts, axis=1).reshape(WIDE, 128)

    def turn(h, carry):
        a, b = 2 * h, 2 * h + 1
        one, two = xd[0:LEAVES, a], xd[0:LEAVES, b]
        cols = [pl.ds(pl.multiple_of(plane * WIDE, 128), WIDE) for plane in (a, b)]
        side = lax.broadcasted_iota(jnp.int32, (WIDE, 128), 1) < CH
        rolled = [pltpu.roll(one, CH, 3), pltpu.roll(two, CH, 3)]
        for n, field in enumerate((one, two)):
            both = jnp.where(side, spread(rolled[n], -1), spread(field, 0))
            zt[0 : 2 * CH, cols[n]] = both.astype(BF16).T
        both = jnp.where(side, spread(rolled[0], 1), spread(two, 1)).astype(BF16).T
        zt[2 * CH :, cols[0]] = both[:CH]
        zt[2 * CH :, cols[1]] = both[CH:]
        return carry

    def planes(p, a, count):
        right = jnp.concatenate(
            [
                a0[pl.ds(a + p + 1, count)].reshape(count * WIDE, 128),
                a2[pl.ds(a + p + 1, count)].reshape(count * WIDE, 128),
            ],
            axis=1,
        )
        cols = pl.ds(pl.multiple_of(a * WIDE, 128), count * WIDE)
        return jnp.dot(zt[:, cols], right, preferred_element_type=F32)

    def gradient(n, p, start, pairs):
        total = lax.fori_loop(
            0,
            pairs,
            lambda h, t: t + planes(p, start + 2 * h, 2),
            jnp.zeros((3 * CH, 256), F32),
        )
        if pairs < 4:
            total = total + planes(p, start + 2 * pairs, 1)
        sums[n] = total

    def lay(n):
        g[...] = sums[n].T

        def put(t, value):
            part[n, t // 18, t % 18 // per, t % 18 % per] = value

        for t in range(24):
            put(t, g[8 * t : 8 * t + 8, 0:128])
        ahead = jnp.concatenate([g[0:CH, 128:], g[CH : 2 * CH, 128:]], axis=1)
        for t in range(8):
            put(24 + t, ahead[8 * t : 8 * t + 8])
        ahead = jnp.concatenate([g[2 * CH : 160, 128:], g[160:192, 128:]], axis=1)
        for t in range(4):
            put(32 + t, ahead[8 * t : 8 * t + 8])

    def give(n, p):
        for t in range(36):
            value = full[n, t // 18, t % 18 // per, t % 18 % per]
            if t < 24:
                r, rows = t // 8 - 1, slice(t % 8 * 8, t % 8 * 8 + 8)
                grad_ref[tap(p, -1, r), rows] = value[:, :CH]
                grad_ref[tap(p, 0, r), rows] = value[:, CH:]
            elif t < 32:
                rows = slice((t - 24) * 8, (t - 24) * 8 + 8)
                grad_ref[tap(p, 1, -1), rows] = value[:, :CH]
                grad_ref[tap(p, 1, 0), rows] = value[:, CH:]
            else:
                at_row = (t - 32) * 8
                grad_ref[tap(p, 1, 1), at_row : at_row + 8] = value[:, :CH]
                grad_ref[tap(p, 1, 1), 32 + at_row : 40 + at_row] = value[:, CH:]

    def pair(n):
        return copy_to(part.at[n, 1 - core], mates.at[n], core_sems.at[0, n], core_sems.at[1, n], mate)

    def pair_back(n):
        whole = full.at[n, core]
        return copy_to(whole, whole, core_sems.at[2, n], core_sems.at[3, n], mate)

    def scatter(n, to, j):
        k = lax.rem(to - cell + cells, cells)
        return copy_to(
            summed.at[n, j], terms.at[n, k], scatter_sent.at[n], scatter_got.at[n], to * 2 + core
        )

    def gather(n, k, j):
        to = lax.rem(cell + k, cells)
        return copy_to(
            own.at[n], full.at[n, core, j], gather_sent.at[n], gather_got.at[n], to * 2 + core
        )

    def whole(ref, sent, got):
        return copy_to(ref, ref, sent, got, mate)

    def owning(n, do):
        j = mine(n)

        @pl.when(j < groups)
        def _():
            do(True, j)

        @pl.when(j >= groups)
        def _():
            do(False, j)

    def scatter_sent_wait(n):
        def do(owns, j):
            ref = summed.at[n, pl.ds(0, groups - owns)]
            whole(ref, scatter_sent.at[n], scatter_got.at[n]).wait_send()

        owning(n, do)

    def gather_got_wait(n):
        def do(owns, j):
            ref = full.at[n, core, pl.ds(0, groups - owns)]
            whole(ref, gather_sent.at[n], gather_got.at[n]).wait_recv()

        owning(n, do)

    def gather_sent_wait(n):
        @pl.when(mine(n) < groups)
        def _():
            ref = terms.at[n, pl.ds(1, cells - 1)]
            whole(ref, gather_sent.at[n], gather_got.at[n]).wait_send()

    def far_first(do):
        def step(k, carry):
            do(k)
            return carry

        lax.fori_loop(1, cells, step, 0)

    def mine(n):
        return lax.rem(cell - groups * n + 4 * cells, cells)

    def scatter_start(n):
        pair(n).wait()
        summed[n] = part[n, core] + mates[n]

        def send(k):
            to = lax.rem(cell + k, cells)
            j = lax.rem(to - groups * n + 4 * cells, cells)

            @pl.when(j < groups)
            def _():
                scatter(n, to, j).start()

        far_first(send)

    def gather_start(n):
        j = mine(n)

        @pl.when(j < groups)
        def _():
            total = summed[n, j]
            whole(terms.at[n, pl.ds(1, cells - 1)], scatter_sent.at[n], scatter_got.at[n]).wait_recv()
            for k in range(1, cells):
                total = total + terms[n, k]
            own[n] = total * scale
            far_first(lambda k: gather(n, k, j).start())
            full[n, core, j] = own[n]

    def pair_back_start(n):
        gather_got_wait(n)
        pair_back(n).start()

    def finish(n, p):
        pair_back(n).wait()
        give(n, p)

    fetches[3].wait()
    def local(h, carry):
        turn(h, carry)
        inner(2 * h, carry)
        inner(2 * h + 1, carry)
        return carry

    lax.fori_loop(0, LEAVES // 2, local, 0)

    pl.semaphore_wait(barrier, cells + 2)
    copy_up = copy_to(send_high, got_high, halo_sems.at[0, 0], halo_sems.at[0, 1], up)
    copy_down = copy_to(send_low, got_low, halo_sems.at[1, 0], halo_sems.at[1, 1], down)
    copy_up.start()
    copy_down.start()
    gradient(0, 0, 0, 4)
    lay(0)
    pair(0).start()
    gradient(1, -1, 1, 3)
    gradient(2, 1, 0, 3)
    scatter_start(0)
    copy_up.wait()
    copy_down.wait()
    for s in range(LEAVES):
        high[LEAVES + s] = got_high[s].astype(F32).reshape(SIDE, SIDE, 128)
        low[LEAVES + s] = got_low[s].astype(F32).reshape(SIDE, SIDE, 128)

    def outer(s, carry):
        for p, row, pool in ((-1, 0, high), (1, SIDE + 1, low)):
            ids = {(q + 1, r + 1): source(s, p, q, r) for q in (-1, 0, 1) for r in (-1, 0, 1)}
            build(s, row, lambda i, lo, hi, pool=pool: pool[i, lo:hi], ids)
        return carry

    lax.fori_loop(0, LEAVES, outer, 0)

    half = lax.broadcasted_iota(jnp.int32, (WIDE, 128), 1) < CH

    def convolve(s, carry):
        xs, ds = [], []
        for n in range(3):
            one = a0[n : n + SIDE, s].reshape(WIDE, 128)
            two = a1[n : n + SIDE, s].reshape(WIDE, 128)
            three = a2[n : n + SIDE, s].reshape(WIDE, 128)
            xs += [one, three]
            ds += [two, three]
        yo = jnp.dot(jnp.concatenate(xs, axis=1), wf[...], preferred_element_type=F32)
        yb = jnp.dot(jnp.concatenate(ds, axis=1), wb[...], preferred_element_type=F32)
        shape = (SIDE, 10, SIDE, 128)
        ahead = (yo[:, 128:] + yb[:, 128:]).reshape(shape)
        behind = jnp.where(half, yo[:, :128], yb[:, :128]).reshape(shape)
        level = pltpu.roll(jnp.where(half, yb[:, :128], yo[:, :128]), CH, 1).reshape(shape)
        total = behind[:, 0:8] + level[:, 1:9] + ahead[:, 2:10]
        turned = total.reshape(VOX, 128).T * occ[s]
        out_ref[s] = turned[:CH].astype(BF16)
        back_ref[s] = turned[CH:].astype(BF16)
        return carry

    sums[1] += planes(-1, 0, 1)
    lay(1)
    pair(1).start()
    sums[2] += planes(1, SIDE - 1, 1)
    lay(2)
    pair(2).start()

    fetches[4].wait()

    def weight(p, q, r):
        return w_ref[tap(p, q, r)].astype(F32)

    for n, p in enumerate((-1, 0, 1)):
        rows = []
        for r in (-1, 0, 1):
            rows.append(
                jnp.concatenate([weight(p, -1, r), weight(p, 0, r), weight(p, 1, r), none], axis=1)
            )
        rows.append(jnp.zeros((CH, 4 * CH), F32))
        wf[n * 256 : (n + 1) * 256] = jnp.concatenate(rows, axis=0).astype(BF16)
        cols = []
        for q in (0, -1, None, 1):
            if q is None:
                cols.append(jnp.zeros((CH, 4 * CH), F32))
            else:
                cols.append(
                    jnp.concatenate(
                        [weight(-p, -q, 0), weight(-p, -q, 1), none, weight(-p, -q, -1)], axis=1
                    )
                )
        wb[n * 256 : (n + 1) * 256] = jnp.concatenate(cols, axis=0).T.astype(BF16)

    scatter_start(1)
    scatter_start(2)
    gather_start(0)
    lax.fori_loop(0, 6, convolve, 0)
    gather_start(1)
    gather_start(2)
    lax.fori_loop(6, 8, convolve, 0)
    leave = [
        pltpu.make_async_copy(out_ref, out_hbm, out_sems.at[0]),
        pltpu.make_async_copy(back_ref, back_hbm, out_sems.at[1]),
    ]
    leave[0].start()
    leave[1].start()

    def grad_leave(n, p):
        rows = pl.ds(9 * (p + 1), 9)
        leave.append(
            pltpu.make_async_copy(grad_ref.at[rows], grad_hbm.at[rows], out_sems.at[2 + n])
        )
        leave[-1].start()

    for n in range(3):
        scatter_sent_wait(n)
    pair_back_start(0)
    finish(0, 0)
    grad_leave(0, 0)
    pair_back_start(1)
    pair_back_start(2)
    for n in range(3):
        gather_sent_wait(n)
    finish(1, -1)
    grad_leave(1, -1)
    finish(2, 1)
    grad_leave(2, 1)
    for copy in leave:
        copy.wait()


PIECES = ((0, 0, 4), (0, 4, 4), (1, 0, 4), (1, 4, 4), (2, 0, 9), (2, 9, 9), (2, 18, 9))


def write_out(*refs):
    sems = refs[9]
    ins, outs = [], []
    for n, (which, start, count) in enumerate(PIECES):
        rows = pl.ds(start, count)
        source, dest, held = (refs[which + m].at[rows] for m in (0, 3, 6))
        ins.append(pltpu.make_async_copy(source, held, sems.at[0, n]))
        outs.append(pltpu.make_async_copy(held, dest, sems.at[1, n]))
    for copy in ins:
        copy.start()
    for n, copy in enumerate(ins):
        copy.wait()
        outs[n].start()
    for copy in outs:
        copy.wait()


def shards(cells, features, cotangent, weight, mask_words, neighbors):
    scale = float(cells * 2 * LEAVES * VOX) ** -0.5
    vmem = pltpu.VMEM
    dma = pltpu.SemaphoreType.DMA
    in_hbm = pl.BlockSpec(memory_space=pltpu.HBM)
    field = jax.ShapeDtypeStruct((LEAVES, CH, VOX), BF16)
    results = (field, field, jax.ShapeDtypeStruct((27, CH, CH), F32))
    per = -(-18 // cells)
    groups = 18 // per
    tiles = (groups, per, 8, 128)
    made = pl.pallas_call(
        functools.partial(kernel, cells, scale),
        out_shape=results,
        in_specs=[in_hbm] * 5,
        out_specs=(in_hbm,) * 3,
        scratch_shapes=[
            vmem((LEAVES, CH, VOX), BF16),
            vmem((LEAVES, CH, VOX), BF16),
            vmem((27, CH, CH), F32),
            vmem((LEAVES, CH, VOX), BF16),
            vmem((LEAVES, CH, VOX), BF16),
            vmem((27, CH, CH), BF16),
            vmem(mask_words.shape, jnp.int32),
            pltpu.SMEM(neighbors.shape, jnp.int32),
            vmem((LEAVES, 1, VOX), F32),
            vmem((LEAVES + 1, SIDE, SIDE, SIDE, 128), F32),
            vmem((2 * LEAVES + 1, SIDE, SIDE, 128), F32),
            vmem((2 * LEAVES + 1, SIDE, SIDE, 128), F32),
            vmem((LEAVES, PLANE, 128), BF16),
            vmem((LEAVES, PLANE, 128), BF16),
            vmem((LEAVES, PLANE, 128), BF16),
            vmem((LEAVES, PLANE, 128), BF16),
            vmem((10, LEAVES, ROWS, 128), BF16),
            vmem((10, LEAVES, ROWS, 128), BF16),
            vmem((10, LEAVES, ROWS, 128), BF16),
            vmem((3 * CH, LEAVES * WIDE), BF16),
            vmem((768, 256), BF16),
            vmem((768, 256), BF16),
            vmem((256, 192), F32),
            vmem((3, 192, 256), F32),
            vmem((3, 2) + tiles, F32),
            vmem((3,) + tiles, F32),
            vmem((3,) + tiles, F32),
            vmem((3, cells) + tiles[1:], F32),
            vmem((3,) + tiles[1:], F32),
            vmem((3, 2) + tiles, F32),
            dma((5,)),
            dma((5,)),
            dma((2, 2)),
            dma((4, 3)),
            dma((3,)),
            dma((3,)),
            dma((3,)),
            dma((3,)),
        ],
        compiler_params=pltpu.CompilerParams(
            collective_id=0, has_side_effects=True, vmem_limit_bytes=60_000_000
        ),
        name="sparse_conv",
    )(features, cotangent, weight, mask_words, neighbors)
    return pl.pallas_call(
        write_out,
        out_shape=results,
        in_specs=[in_hbm] * 3,
        out_specs=(in_hbm,) * 3,
        scratch_shapes=[vmem(r.shape, r.dtype) for r in results] + [dma((2, len(PIECES)))],
        compiler_params=pltpu.CompilerParams(vmem_limit_bytes=60_000_000),
        name="write_out",
    )(*made)


def solution(mesh):
    placed = (
        P(("scene", "dom"), None, None),
        P(("scene", "dom"), None, None),
        P(),
        P(("scene", "dom"), None),
        P(("scene", "dom"), None),
    )
    return jax.shard_map(
        functools.partial(shards, mesh.shape["dom"] // 2),
        mesh=mesh,
        in_specs=placed,
        out_specs=(
            P(("scene", "dom"), None, None),
            P(("scene", "dom"), None, None),
            P("scene", None, None),
        ),
        check_vma=False,
    )
```

```python
import functools

import jax
import jax.numpy as jnp
from jax import lax
from jax.experimental import pallas as pl
from jax.experimental.pallas import tpu as pltpu
from jax.sharding import PartitionSpec as P

LEAVES = 8
CH = 64
SIDE = 8
VOX = 512
PLANE = 64
ROWS = 80
WIDE = 640
MESH = pl.DeviceIdType.MESH
F32 = jnp.float32
BF16 = jnp.bfloat16


def tap(p, q, r):
    return 9 * (p + 1) + 3 * (q + 1) + r + 1


def copy_to(src, dst, send, recv, dom):
    return pltpu.make_async_remote_copy(
        src_ref=src,
        dst_ref=dst,
        send_sem=send,
        recv_sem=recv,
        device_id={"dom": dom},
        device_id_type=MESH,
    )


def kernel(
    cells,
    scale,
    x_hbm,
    dy_hbm,
    w_hbm,
    words_hbm,
    near_hbm,
    out_hbm,
    back_hbm,
    grad_hbm,
    out_ref,
    back_ref,
    grad_ref,
    x_ref,
    dy_ref,
    w_ref,
    words_ref,
    near_ref,
    occ,
    xd,
    high,
    low,
    send_high,
    send_low,
    got_high,
    got_low,
    a0,
    a1,
    a2,
    zt,
    wf,
    wb,
    g,
    sums,
    part,
    mates,
    summed,
    terms,
    own,
    full,
    in_sems,
    out_sems,
    halo_sems,
    core_sems,
    scatter_sent,
    scatter_got,
    gather_sent,
    gather_got,
):
    ndom = cells * 2
    dom = lax.axis_index("dom")
    core = lax.rem(dom, 2)
    cell = lax.div(dom, 2)
    up = lax.rem(dom + 1, ndom)
    down = lax.rem(dom + ndom - 1, ndom)
    mate = dom + 1 - 2 * core
    groups, per = part.shape[2:4]
    middle = cells // 2 + 2

    fetches = [
        pltpu.make_async_copy(source, dest, in_sems.at[n])
        for n, (source, dest) in enumerate(
            (
                (words_hbm, words_ref),
                (x_hbm, x_ref),
                (dy_hbm, dy_ref),
                (near_hbm, near_ref),
                (w_hbm, w_ref),
            )
        )
    ]
    for fetch in fetches:
        fetch.start()

    barrier = pltpu.get_barrier_semaphore()

    def greet(k, carry):
        to = lax.rem(cell + k, cells) * 2 + core
        pl.semaphore_signal(barrier, inc=1, device_id={"dom": to}, device_id_type=MESH)
        return carry

    for d in (up, down, mate):
        pl.semaphore_signal(barrier, inc=1, device_id={"dom": d}, device_id_type=MESH)
    lax.fori_loop(1, cells, greet, 0)
    fetches[0].wait()

    at = lax.broadcasted_iota(jnp.int32, (LEAVES, VOX), 1)
    word_at = lax.shift_right_logical(at * 2185, 16)
    bit_at = at - 30 * word_at
    words = jnp.zeros((LEAVES, VOX), jnp.int32)
    for n in range(18):
        words = jnp.where(word_at == n, words_ref[:, n : n + 1], words)
    bits = (lax.shift_right_logical(words, bit_at) & 1).astype(F32)
    for s in range(LEAVES):
        occ[s] = bits[s : s + 1]

    def prepare(s, carry):
        both = jnp.concatenate([x_ref[s].astype(F32), dy_ref[s].astype(F32)], axis=0)
        turned = (both * occ[s]).T.reshape(SIDE, SIDE, SIDE, 128)
        xd[s] = turned
        high[s] = turned[SIDE - 1]
        low[s] = turned[0]
        send_high[s] = turned[SIDE - 1].reshape(PLANE, 128).astype(BF16)
        send_low[s] = turned[0].reshape(PLANE, 128).astype(BF16)
        return carry

    fetches[1].wait()
    fetches[2].wait()
    lax.fori_loop(0, LEAVES, prepare, 0)
    xd[LEAVES] = jnp.zeros((SIDE, SIDE, SIDE, 128), F32)
    high[2 * LEAVES] = jnp.zeros((SIDE, SIDE, 128), F32)
    low[2 * LEAVES] = jnp.zeros((SIDE, SIDE, 128), F32)


    none = jnp.zeros((CH, CH), F32)
    sub = lax.broadcasted_iota(jnp.int32, (10, SIDE, 128), 1)
    lane = lax.broadcasted_iota(jnp.int32, (10, SIDE, 128), 2)
    left = lane < CH
    first, last = sub == 0, sub == SIDE - 1

    def source(s, p, q, r):
        t = tap(p, q, r)
        if t == 13:
            return s
        n = near_ref[s, t if t < 13 else t - 1]
        slot = n & 7
        if p == 0:
            return jnp.where(n < 0, LEAVES, slot)
        here = lax.shift_right_arithmetic(n, 3) == dom
        return jnp.where(n < 0, 2 * LEAVES, jnp.where(here, slot, LEAVES + slot))

    def build(s, row, pool, ids):
        def line(r):
            return jnp.concatenate(
                [pool(ids[0, r], SIDE - 1, SIDE), pool(ids[1, r], 0, SIDE), pool(ids[2, r], 0, 1)],
                axis=0,
            )

        mid, before, after = line(1), line(0), line(2)
        less = pltpu.roll(jnp.where(last, before, mid), 1, 1)
        more = pltpu.roll(jnp.where(first, after, mid), SIDE - 1, 1)
        swapped = pltpu.roll(mid, CH, 2)
        a0[row, s] = jnp.where(left, less, swapped).reshape(ROWS, 128).astype(BF16)
        a1[row, s] = jnp.where(left, swapped, less).reshape(ROWS, 128).astype(BF16)
        a2[row, s] = more.reshape(ROWS, 128).astype(BF16)

    def inner(s, carry):
        ids = {(q + 1, r + 1): source(s, 0, q, r) for q in (-1, 0, 1) for r in (-1, 0, 1)}
        for a in range(SIDE):
            build(s, a + 1, lambda i, lo, hi, a=a: xd[i, a, lo:hi], ids)
        return carry

    gap = jnp.zeros((LEAVES, 1, SIDE, 128), F32)

    def spread(field, q):
        parts = [gap, gap]
        parts.insert(q + 1, field)
        return jnp.concatenate(parts, axis=1).reshape(WIDE, 128)

    def turn(h, carry):
        a, b = 2 * h, 2 * h + 1
        one, two = xd[0:LEAVES, a], xd[0:LEAVES, b]
        cols = [pl.ds(pl.multiple_of(plane * WIDE, 128), WIDE) for plane in (a, b)]
        side = lax.broadcasted_iota(jnp.int32, (WIDE, 128), 1) < CH
        rolled = [pltpu.roll(one, CH, 3), pltpu.roll(two, CH, 3)]
        for n, field in enumerate((one, two)):
            both = jnp.where(side, spread(rolled[n], -1), spread(field, 0))
            zt[0 : 2 * CH, cols[n]] = both.astype(BF16).T
        both = jnp.where(side, spread(rolled[0], 1), spread(two, 1)).astype(BF16).T
        zt[2 * CH :, cols[0]] = both[:CH]
        zt[2 * CH :, cols[1]] = both[CH:]
        return carry

    def planes(p, a, count):
        right = jnp.concatenate(
            [
                a0[pl.ds(a + p + 1, count)].reshape(count * WIDE, 128),
                a2[pl.ds(a + p + 1, count)].reshape(count * WIDE, 128),
            ],
            axis=1,
        )
        cols = pl.ds(pl.multiple_of(a * WIDE, 128), count * WIDE)
        return jnp.dot(zt[:, cols], right, preferred_element_type=F32)

    def gradient(n, p, start, pairs):
        total = lax.fori_loop(
            0,
            pairs,
            lambda h, t: t + planes(p, start + 2 * h, 2),
            jnp.zeros((3 * CH, 256), F32),
        )
        if pairs < 4:
            total = total + planes(p, start + 2 * pairs, 1)
        sums[n] = total

    def lay(n):
        g[...] = sums[n].T

        def put(t, value):
            part[n, t // 18, t % 18 // per, t % 18 % per] = value

        for t in range(24):
            put(t, g[8 * t : 8 * t + 8, 0:128])
        ahead = jnp.concatenate([g[0:CH, 128:], g[CH : 2 * CH, 128:]], axis=1)
        for t in range(8):
            put(24 + t, ahead[8 * t : 8 * t + 8])
        ahead = jnp.concatenate([g[2 * CH : 160, 128:], g[160:192, 128:]], axis=1)
        for t in range(4):
            put(32 + t, ahead[8 * t : 8 * t + 8])

    def give(n, p):
        for t in range(36):
            value = full[n, t // 18, t % 18 // per, t % 18 % per]
            if t < 24:
                r, rows = t // 8 - 1, slice(t % 8 * 8, t % 8 * 8 + 8)
                grad_ref[tap(p, -1, r), rows] = value[:, :CH]
                grad_ref[tap(p, 0, r), rows] = value[:, CH:]
            elif t < 32:
                rows = slice((t - 24) * 8, (t - 24) * 8 + 8)
                grad_ref[tap(p, 1, -1), rows] = value[:, :CH]
                grad_ref[tap(p, 1, 0), rows] = value[:, CH:]
            else:
                at_row = (t - 32) * 8
                grad_ref[tap(p, 1, 1), at_row : at_row + 8] = value[:, :CH]
                grad_ref[tap(p, 1, 1), 32 + at_row : 40 + at_row] = value[:, CH:]

    def pair(n):
        return copy_to(part.at[n, 1 - core], mates.at[n], core_sems.at[0, n], core_sems.at[1, n], mate)

    def pair_back(n):
        whole = full.at[n, core]
        return copy_to(whole, whole, core_sems.at[2, n], core_sems.at[3, n], mate)

    def scatter(n, to, j):
        k = lax.rem(to - cell + cells, cells)
        return copy_to(
            summed.at[n, j], terms.at[n, k], scatter_sent.at[n], scatter_got.at[n], to * 2 + core
        )

    def gather(n, k, j):
        to = lax.rem(cell + k, cells)
        return copy_to(
            own.at[n], full.at[n, core, j], gather_sent.at[n], gather_got.at[n], to * 2 + core
        )

    def whole(ref, sent, got):
        return copy_to(ref, ref, sent, got, mate)

    def owning(n, do):
        j = mine(n)

        @pl.when(j < groups)
        def _():
            do(True, j)

        @pl.when(j >= groups)
        def _():
            do(False, j)

    def scatter_sent_wait(n):
        def do(owns, j):
            ref = summed.at[n, pl.ds(0, groups - owns)]
            whole(ref, scatter_sent.at[n], scatter_got.at[n]).wait_send()

        owning(n, do)

    def gather_got_wait(n):
        def do(owns, j):
            ref = full.at[n, core, pl.ds(0, groups - owns)]
            whole(ref, gather_sent.at[n], gather_got.at[n]).wait_recv()

        owning(n, do)

    def gather_sent_wait(n):
        @pl.when(mine(n) < groups)
        def _():
            ref = terms.at[n, pl.ds(1, cells - 1)]
            whole(ref, gather_sent.at[n], gather_got.at[n]).wait_send()

    def far_first(do):
        def step(k, carry):
            do(k)
            return carry

        lax.fori_loop(1, cells, step, 0)

    def mine(n):
        return lax.rem(cell - groups * n + 4 * cells, cells)

    def scatter_start(n):
        pair(n).wait()
        summed[n] = part[n, core] + mates[n]

        def send(k):
            to = lax.rem(cell + k, cells)
            j = lax.rem(to - groups * n + 4 * cells, cells)

            @pl.when(j < groups)
            def _():
                scatter(n, to, j).start()

        far_first(send)

    def gather_start(n):
        j = mine(n)

        @pl.when(j < groups)
        def _():
            total = summed[n, j]
            whole(terms.at[n, pl.ds(1, cells - 1)], scatter_sent.at[n], scatter_got.at[n]).wait_recv()
            for k in range(1, cells):
                total = total + terms[n, k]
            own[n] = total * scale
            far_first(lambda k: gather(n, k, j).start())
            full[n, core, j] = own[n]

    def pair_back_start(n):
        gather_got_wait(n)
        pair_back(n).start()

    def finish(n, p):
        pair_back(n).wait()
        give(n, p)

    fetches[3].wait()
    def local(h, carry):
        turn(h, carry)
        inner(2 * h, carry)
        inner(2 * h + 1, carry)
        return carry

    lax.fori_loop(0, LEAVES // 2, local, 0)

    pl.semaphore_wait(barrier, cells + 2)
    copy_up = copy_to(send_high, got_high, halo_sems.at[0, 0], halo_sems.at[0, 1], up)
    copy_down = copy_to(send_low, got_low, halo_sems.at[1, 0], halo_sems.at[1, 1], down)
    copy_up.start()
    copy_down.start()
    gradient(0, 0, 0, 4)
    lay(0)
    pair(0).start()
    gradient(1, -1, 1, 3)
    gradient(2, 1, 0, 3)
    scatter_start(0)
    copy_up.wait()
    copy_down.wait()
    for s in range(LEAVES):
        high[LEAVES + s] = got_high[s].astype(F32).reshape(SIDE, SIDE, 128)
        low[LEAVES + s] = got_low[s].astype(F32).reshape(SIDE, SIDE, 128)

    def outer(s, carry):
        for p, row, pool in ((-1, 0, high), (1, SIDE + 1, low)):
            ids = {(q + 1, r + 1): source(s, p, q, r) for q in (-1, 0, 1) for r in (-1, 0, 1)}
            build(s, row, lambda i, lo, hi, pool=pool: pool[i, lo:hi], ids)
        return carry

    lax.fori_loop(0, LEAVES, outer, 0)

    half = lax.broadcasted_iota(jnp.int32, (WIDE, 128), 1) < CH

    def convolve(s, carry):
        xs, ds = [], []
        for n in range(3):
            one = a0[n : n + SIDE, s].reshape(WIDE, 128)
            two = a1[n : n + SIDE, s].reshape(WIDE, 128)
            three = a2[n : n + SIDE, s].reshape(WIDE, 128)
            xs += [one, three]
            ds += [two, three]
        yo = jnp.dot(jnp.concatenate(xs, axis=1), wf[...], preferred_element_type=F32)
        yb = jnp.dot(jnp.concatenate(ds, axis=1), wb[...], preferred_element_type=F32)
        shape = (SIDE, 10, SIDE, 128)
        ahead = (yo[:, 128:] + yb[:, 128:]).reshape(shape)
        behind = jnp.where(half, yo[:, :128], yb[:, :128]).reshape(shape)
        level = pltpu.roll(jnp.where(half, yb[:, :128], yo[:, :128]), CH, 1).reshape(shape)
        total = behind[:, 0:8] + level[:, 1:9] + ahead[:, 2:10]
        turned = total.reshape(VOX, 128).T * occ[s]
        out_ref[s] = turned[:CH].astype(BF16)
        back_ref[s] = turned[CH:].astype(BF16)
        return carry

    sums[1] += planes(-1, 0, 1)
    lay(1)
    pair(1).start()
    sums[2] += planes(1, SIDE - 1, 1)
    lay(2)
    pair(2).start()

    scatter_start(1)
    scatter_start(2)
    fetches[4].wait()

    def weight(p, q, r):
        return w_ref[tap(p, q, r)].astype(F32)

    for n, p in enumerate((-1, 0, 1)):
        rows = []
        for r in (-1, 0, 1):
            rows.append(
                jnp.concatenate([weight(p, -1, r), weight(p, 0, r), weight(p, 1, r), none], axis=1)
            )
        rows.append(jnp.zeros((CH, 4 * CH), F32))
        wf[n * 256 : (n + 1) * 256] = jnp.concatenate(rows, axis=0).astype(BF16)
        cols = []
        for q in (0, -1, None, 1):
            if q is None:
                cols.append(jnp.zeros((CH, 4 * CH), F32))
            else:
                cols.append(
                    jnp.concatenate(
                        [weight(-p, -q, 0), weight(-p, -q, 1), none, weight(-p, -q, -1)], axis=1
                    )
                )
        wb[n * 256 : (n + 1) * 256] = jnp.concatenate(cols, axis=0).T.astype(BF16)

    gather_start(0)
    lax.fori_loop(0, 6, convolve, 0)
    gather_start(1)
    gather_start(2)
    lax.fori_loop(6, 8, convolve, 0)
    leave = [
        pltpu.make_async_copy(out_ref, out_hbm, out_sems.at[0]),
        pltpu.make_async_copy(back_ref, back_hbm, out_sems.at[1]),
    ]
    leave[0].start()
    leave[1].start()

    def grad_leave(n, p):
        rows = pl.ds(9 * (p + 1), 9)
        leave.append(
            pltpu.make_async_copy(grad_ref.at[rows], grad_hbm.at[rows], out_sems.at[2 + n])
        )
        leave[-1].start()

    for n in range(3):
        scatter_sent_wait(n)
    pair_back_start(0)
    finish(0, 0)
    grad_leave(0, 0)
    pair_back_start(1)
    pair_back_start(2)
    for n in range(3):
        gather_sent_wait(n)
    finish(1, -1)
    grad_leave(1, -1)
    finish(2, 1)
    grad_leave(2, 1)
    for copy in leave:
        copy.wait()


def write_out(*refs):
    sems = refs[6]
    copies = [pltpu.make_async_copy(refs[n], refs[n + 3], sems.at[n]) for n in range(3)]
    for copy in copies:
        copy.start()
    for copy in copies:
        copy.wait()


def shards(cells, features, cotangent, weight, mask_words, neighbors):
    scale = float(cells * 2 * LEAVES * VOX) ** -0.5
    vmem = pltpu.VMEM
    dma = pltpu.SemaphoreType.DMA
    in_hbm = pl.BlockSpec(memory_space=pltpu.HBM)
    anywhere = pl.BlockSpec(memory_space=pl.ANY)
    field = jax.ShapeDtypeStruct((LEAVES, CH, VOX), BF16)
    results = (field, field, jax.ShapeDtypeStruct((27, CH, CH), F32))
    per = -(-18 // cells)
    groups = 18 // per
    tiles = (groups, per, 8, 128)
    made = pl.pallas_call(
        functools.partial(kernel, cells, scale),
        out_shape=results,
        in_specs=[in_hbm] * 5,
        out_specs=(anywhere,) * 3,
        scratch_shapes=[
            vmem((LEAVES, CH, VOX), BF16),
            vmem((LEAVES, CH, VOX), BF16),
            vmem((27, CH, CH), F32),
            vmem((LEAVES, CH, VOX), BF16),
            vmem((LEAVES, CH, VOX), BF16),
            vmem((27, CH, CH), BF16),
            vmem(mask_words.shape, jnp.int32),
            pltpu.SMEM(neighbors.shape, jnp.int32),
            vmem((LEAVES, 1, VOX), F32),
            vmem((LEAVES + 1, SIDE, SIDE, SIDE, 128), F32),
            vmem((2 * LEAVES + 1, SIDE, SIDE, 128), F32),
            vmem((2 * LEAVES + 1, SIDE, SIDE, 128), F32),
            vmem((LEAVES, PLANE, 128), BF16),
            vmem((LEAVES, PLANE, 128), BF16),
            vmem((LEAVES, PLANE, 128), BF16),
            vmem((LEAVES, PLANE, 128), BF16),
            vmem((10, LEAVES, ROWS, 128), BF16),
            vmem((10, LEAVES, ROWS, 128), BF16),
            vmem((10, LEAVES, ROWS, 128), BF16),
            vmem((3 * CH, LEAVES * WIDE), BF16),
            vmem((768, 256), BF16),
            vmem((768, 256), BF16),
            vmem((256, 192), F32),
            vmem((3, 192, 256), F32),
            vmem((3, 2) + tiles, F32),
            vmem((3,) + tiles, F32),
            vmem((3,) + tiles, F32),
            vmem((3, cells) + tiles[1:], F32),
            vmem((3,) + tiles[1:], F32),
            vmem((3, 2) + tiles, F32),
            dma((5,)),
            dma((5,)),
            dma((2, 2)),
            dma((4, 3)),
            dma((3,)),
            dma((3,)),
            dma((3,)),
            dma((3,)),
        ],
        compiler_params=pltpu.CompilerParams(
            collective_id=0, has_side_effects=True, vmem_limit_bytes=54_000_000
        ),
        name="sparse_conv",
    )(*(pltpu.with_memory_space_constraint(a, pltpu.HBM) for a in (features, cotangent, weight, mask_words, neighbors)))
    return pl.pallas_call(
        write_out,
        out_shape=results,
        in_specs=[anywhere] * 3,
        out_specs=(in_hbm,) * 3,
        scratch_shapes=[dma((3,))],
        compiler_params=pltpu.CompilerParams(vmem_limit_bytes=1_000_000),
        name="write_out",
    )(*made)


def solution(mesh):
    placed = (
        P(("scene", "dom"), None, None),
        P(("scene", "dom"), None, None),
        P(),
        P(("scene", "dom"), None),
        P(("scene", "dom"), None),
    )
    return jax.shard_map(
        functools.partial(shards, mesh.shape["dom"] // 2),
        mesh=mesh,
        in_specs=placed,
        out_specs=(
            P(("scene", "dom"), None, None),
            P(("scene", "dom"), None, None),
            P("scene", None, None),
        ),
        check_vma=False,
    )
```

```python
import functools

import jax
import jax.numpy as jnp
from jax import lax
from jax.experimental import pallas as pl
from jax.experimental.pallas import tpu as pltpu
from jax.sharding import PartitionSpec as P

LEAVES = 8
CH = 64
SIDE = 8
VOX = 512
PLANE = 64
ROWS = 80
WIDE = 640
MESH = pl.DeviceIdType.MESH
F32 = jnp.float32
BF16 = jnp.bfloat16


def tap(p, q, r):
    return 9 * (p + 1) + 3 * (q + 1) + r + 1


def copy_to(src, dst, send, recv, dom):
    return pltpu.make_async_remote_copy(
        src_ref=src,
        dst_ref=dst,
        send_sem=send,
        recv_sem=recv,
        device_id={"dom": dom},
        device_id_type=MESH,
    )


def kernel(
    cells,
    scale,
    x_hbm,
    dy_hbm,
    w_hbm,
    words_hbm,
    near_hbm,
    out_ref,
    back_ref,
    grad_ref,
    x_ref,
    dy_ref,
    w_ref,
    words_ref,
    near_ref,
    occ,
    xd,
    high,
    low,
    send_high,
    send_low,
    got_high,
    got_low,
    a0,
    a1,
    a2,
    zt,
    wf,
    wb,
    g,
    sums,
    part,
    mates,
    summed,
    terms,
    own,
    full,
    in_sems,
    halo_sems,
    core_sems,
    scatter_sent,
    scatter_got,
    gather_sent,
    gather_got,
):
    ndom = cells * 2
    dom = lax.axis_index("dom")
    core = lax.rem(dom, 2)
    cell = lax.div(dom, 2)
    up = lax.rem(dom + 1, ndom)
    down = lax.rem(dom + ndom - 1, ndom)
    mate = dom + 1 - 2 * core
    groups, per = part.shape[2:4]
    middle = cells // 2 + 2

    fetches = [
        pltpu.make_async_copy(source, dest, in_sems.at[n])
        for n, (source, dest) in enumerate(
            (
                (words_hbm, words_ref),
                (x_hbm, x_ref),
                (dy_hbm, dy_ref),
                (near_hbm, near_ref),
                (w_hbm, w_ref),
            )
        )
    ]
    for fetch in fetches:
        fetch.start()

    barrier = pltpu.get_barrier_semaphore()

    def greet(k, carry):
        to = lax.rem(cell + k, cells) * 2 + core
        pl.semaphore_signal(barrier, inc=1, device_id={"dom": to}, device_id_type=MESH)
        return carry

    for d in (up, down, mate):
        pl.semaphore_signal(barrier, inc=1, device_id={"dom": d}, device_id_type=MESH)
    lax.fori_loop(1, cells, greet, 0)
    fetches[0].wait()

    at = lax.broadcasted_iota(jnp.int32, (LEAVES, VOX), 1)
    word_at = lax.shift_right_logical(at * 2185, 16)
    bit_at = at - 30 * word_at
    words = jnp.zeros((LEAVES, VOX), jnp.int32)
    for n in range(18):
        words = jnp.where(word_at == n, words_ref[:, n : n + 1], words)
    bits = (lax.shift_right_logical(words, bit_at) & 1).astype(F32)
    for s in range(LEAVES):
        occ[s] = bits[s : s + 1]

    def prepare(s, carry):
        both = jnp.concatenate([x_ref[s].astype(F32), dy_ref[s].astype(F32)], axis=0)
        turned = (both * occ[s]).T.reshape(SIDE, SIDE, SIDE, 128)
        xd[s] = turned
        high[s] = turned[SIDE - 1]
        low[s] = turned[0]
        send_high[s] = turned[SIDE - 1].reshape(PLANE, 128).astype(BF16)
        send_low[s] = turned[0].reshape(PLANE, 128).astype(BF16)
        return carry

    fetches[1].wait()
    fetches[2].wait()
    lax.fori_loop(0, LEAVES, prepare, 0)
    xd[LEAVES] = jnp.zeros((SIDE, SIDE, SIDE, 128), F32)
    high[2 * LEAVES] = jnp.zeros((SIDE, SIDE, 128), F32)
    low[2 * LEAVES] = jnp.zeros((SIDE, SIDE, 128), F32)


    none = jnp.zeros((CH, CH), F32)
    sub = lax.broadcasted_iota(jnp.int32, (10, SIDE, 128), 1)
    lane = lax.broadcasted_iota(jnp.int32, (10, SIDE, 128), 2)
    left = lane < CH
    first, last = sub == 0, sub == SIDE - 1

    def source(s, p, q, r):
        t = tap(p, q, r)
        if t == 13:
            return s
        n = near_ref[s, t if t < 13 else t - 1]
        slot = n & 7
        if p == 0:
            return jnp.where(n < 0, LEAVES, slot)
        here = lax.shift_right_arithmetic(n, 3) == dom
        return jnp.where(n < 0, 2 * LEAVES, jnp.where(here, slot, LEAVES + slot))

    def build(s, row, pool, ids):
        def line(r):
            return jnp.concatenate(
                [pool(ids[0, r], SIDE - 1, SIDE), pool(ids[1, r], 0, SIDE), pool(ids[2, r], 0, 1)],
                axis=0,
            )

        mid, before, after = line(1), line(0), line(2)
        less = pltpu.roll(jnp.where(last, before, mid), 1, 1)
        more = pltpu.roll(jnp.where(first, after, mid), SIDE - 1, 1)
        swapped = pltpu.roll(mid, CH, 2)
        a0[row, s] = jnp.where(left, less, swapped).reshape(ROWS, 128).astype(BF16)
        a1[row, s] = jnp.where(left, swapped, less).reshape(ROWS, 128).astype(BF16)
        a2[row, s] = more.reshape(ROWS, 128).astype(BF16)

    def inner(s, carry):
        ids = {(q + 1, r + 1): source(s, 0, q, r) for q in (-1, 0, 1) for r in (-1, 0, 1)}
        for a in range(SIDE):
            build(s, a + 1, lambda i, lo, hi, a=a: xd[i, a, lo:hi], ids)
        return carry

    gap = jnp.zeros((LEAVES, 1, SIDE, 128), F32)

    def spread(field, q):
        parts = [gap, gap]
        parts.insert(q + 1, field)
        return jnp.concatenate(parts, axis=1).reshape(WIDE, 128)

    def turn(h, carry):
        a, b = 2 * h, 2 * h + 1
        one, two = xd[0:LEAVES, a], xd[0:LEAVES, b]
        cols = [pl.ds(pl.multiple_of(plane * WIDE, 128), WIDE) for plane in (a, b)]
        side = lax.broadcasted_iota(jnp.int32, (WIDE, 128), 1) < CH
        rolled = [pltpu.roll(one, CH, 3), pltpu.roll(two, CH, 3)]
        for n, field in enumerate((one, two)):
            both = jnp.where(side, spread(rolled[n], -1), spread(field, 0))
            zt[0 : 2 * CH, cols[n]] = both.astype(BF16).T
        both = jnp.where(side, spread(rolled[0], 1), spread(two, 1)).astype(BF16).T
        zt[2 * CH :, cols[0]] = both[:CH]
        zt[2 * CH :, cols[1]] = both[CH:]
        return carry

    def planes(p, a, count):
        right = jnp.concatenate(
            [
                a0[pl.ds(a + p + 1, count)].reshape(count * WIDE, 128),
                a2[pl.ds(a + p + 1, count)].reshape(count * WIDE, 128),
            ],
            axis=1,
        )
        cols = pl.ds(pl.multiple_of(a * WIDE, 128), count * WIDE)
        return jnp.dot(zt[:, cols], right, preferred_element_type=F32)

    def gradient(n, p, start, pairs):
        total = lax.fori_loop(
            0,
            pairs,
            lambda h, t: t + planes(p, start + 2 * h, 2),
            jnp.zeros((3 * CH, 256), F32),
        )
        if pairs < 4:
            total = total + planes(p, start + 2 * pairs, 1)
        sums[n] = total

    def lay(n):
        g[...] = sums[n].T

        def put(t, value):
            part[n, t // 18, t % 18 // per, t % 18 % per] = value

        for t in range(24):
            put(t, g[8 * t : 8 * t + 8, 0:128])
        ahead = jnp.concatenate([g[0:CH, 128:], g[CH : 2 * CH, 128:]], axis=1)
        for t in range(8):
            put(24 + t, ahead[8 * t : 8 * t + 8])
        ahead = jnp.concatenate([g[2 * CH : 160, 128:], g[160:192, 128:]], axis=1)
        for t in range(4):
            put(32 + t, ahead[8 * t : 8 * t + 8])

    def give(n, p):
        for t in range(36):
            value = full[n, t // 18, t % 18 // per, t % 18 % per]
            if t < 24:
                r, rows = t // 8 - 1, slice(t % 8 * 8, t % 8 * 8 + 8)
                grad_ref[tap(p, -1, r), rows] = value[:, :CH]
                grad_ref[tap(p, 0, r), rows] = value[:, CH:]
            elif t < 32:
                rows = slice((t - 24) * 8, (t - 24) * 8 + 8)
                grad_ref[tap(p, 1, -1), rows] = value[:, :CH]
                grad_ref[tap(p, 1, 0), rows] = value[:, CH:]
            else:
                at_row = (t - 32) * 8
                grad_ref[tap(p, 1, 1), at_row : at_row + 8] = value[:, :CH]
                grad_ref[tap(p, 1, 1), 32 + at_row : 40 + at_row] = value[:, CH:]

    def pair(n):
        return copy_to(part.at[n, 1 - core], mates.at[n], core_sems.at[0, n], core_sems.at[1, n], mate)

    def pair_back(n):
        whole = full.at[n, core]
        return copy_to(whole, whole, core_sems.at[2, n], core_sems.at[3, n], mate)

    def scatter(n, to, j):
        k = lax.rem(to - cell + cells, cells)
        return copy_to(
            summed.at[n, j], terms.at[n, k], scatter_sent.at[n], scatter_got.at[n], to * 2 + core
        )

    def gather(n, k, j):
        to = lax.rem(cell + k, cells)
        return copy_to(
            own.at[n], full.at[n, core, j], gather_sent.at[n], gather_got.at[n], to * 2 + core
        )

    def whole(ref, sent, got):
        return copy_to(ref, ref, sent, got, mate)

    def owning(n, do):
        j = mine(n)

        @pl.when(j < groups)
        def _():
            do(True, j)

        @pl.when(j >= groups)
        def _():
            do(False, j)

    def scatter_sent_wait(n):
        def do(owns, j):
            ref = summed.at[n, pl.ds(0, groups - owns)]
            whole(ref, scatter_sent.at[n], scatter_got.at[n]).wait_send()

        owning(n, do)

    def gather_got_wait(n):
        def do(owns, j):
            ref = full.at[n, core, pl.ds(0, groups - owns)]
            whole(ref, gather_sent.at[n], gather_got.at[n]).wait_recv()

        owning(n, do)

    def gather_sent_wait(n):
        @pl.when(mine(n) < groups)
        def _():
            ref = terms.at[n, pl.ds(1, cells - 1)]
            whole(ref, gather_sent.at[n], gather_got.at[n]).wait_send()

    def far_first(do):
        def step(k, carry):
            do(k)
            return carry

        lax.fori_loop(1, cells, step, 0)

    def mine(n):
        return lax.rem(cell - groups * n + 4 * cells, cells)

    def scatter_start(n):
        pair(n).wait()
        summed[n] = part[n, core] + mates[n]

        def send(k):
            to = lax.rem(cell + k, cells)
            j = lax.rem(to - groups * n + 4 * cells, cells)

            @pl.when(j < groups)
            def _():
                scatter(n, to, j).start()

        far_first(send)

    def gather_start(n):
        j = mine(n)

        @pl.when(j < groups)
        def _():
            total = summed[n, j]
            whole(terms.at[n, pl.ds(1, cells - 1)], scatter_sent.at[n], scatter_got.at[n]).wait_recv()
            for k in range(1, cells):
                total = total + terms[n, k]
            own[n] = total * scale
            far_first(lambda k: gather(n, k, j).start())
            full[n, core, j] = own[n]

    def pair_back_start(n):
        gather_got_wait(n)
        pair_back(n).start()

    def finish(n, p):
        pair_back(n).wait()
        give(n, p)

    fetches[3].wait()
    def local(h, carry):
        turn(h, carry)
        inner(2 * h, carry)
        inner(2 * h + 1, carry)
        return carry

    lax.fori_loop(0, LEAVES // 2, local, 0)

    pl.semaphore_wait(barrier, cells + 2)
    copy_up = copy_to(send_high, got_high, halo_sems.at[0, 0], halo_sems.at[0, 1], up)
    copy_down = copy_to(send_low, got_low, halo_sems.at[1, 0], halo_sems.at[1, 1], down)
    copy_up.start()
    copy_down.start()
    gradient(0, 0, 0, 4)
    lay(0)
    pair(0).start()
    gradient(1, -1, 1, 3)
    gradient(2, 1, 0, 3)
    scatter_start(0)
    copy_up.wait()
    copy_down.wait()
    for s in range(LEAVES):
        high[LEAVES + s] = got_high[s].astype(F32).reshape(SIDE, SIDE, 128)
        low[LEAVES + s] = got_low[s].astype(F32).reshape(SIDE, SIDE, 128)

    def outer(s, carry):
        for p, row, pool in ((-1, 0, high), (1, SIDE + 1, low)):
            ids = {(q + 1, r + 1): source(s, p, q, r) for q in (-1, 0, 1) for r in (-1, 0, 1)}
            build(s, row, lambda i, lo, hi, pool=pool: pool[i, lo:hi], ids)
        return carry

    lax.fori_loop(0, LEAVES, outer, 0)

    half = lax.broadcasted_iota(jnp.int32, (WIDE, 128), 1) < CH

    def convolve(s, carry):
        xs, ds = [], []
        for n in range(3):
            one = a0[n : n + SIDE, s].reshape(WIDE, 128)
            two = a1[n : n + SIDE, s].reshape(WIDE, 128)
            three = a2[n : n + SIDE, s].reshape(WIDE, 128)
            xs += [one, three]
            ds += [two, three]
        yo = jnp.dot(jnp.concatenate(xs, axis=1), wf[...], preferred_element_type=F32)
        yb = jnp.dot(jnp.concatenate(ds, axis=1), wb[...], preferred_element_type=F32)
        shape = (SIDE, 10, SIDE, 128)
        ahead = (yo[:, 128:] + yb[:, 128:]).reshape(shape)
        behind = jnp.where(half, yo[:, :128], yb[:, :128]).reshape(shape)
        level = pltpu.roll(jnp.where(half, yb[:, :128], yo[:, :128]), CH, 1).reshape(shape)
        total = behind[:, 0:8] + level[:, 1:9] + ahead[:, 2:10]
        turned = total.reshape(VOX, 128).T * occ[s]
        out_ref[s] = turned[:CH].astype(BF16)
        back_ref[s] = turned[CH:].astype(BF16)
        return carry

    sums[1] += planes(-1, 0, 1)
    lay(1)
    pair(1).start()
    sums[2] += planes(1, SIDE - 1, 1)
    lay(2)
    pair(2).start()

    scatter_start(1)
    scatter_start(2)
    fetches[4].wait()

    def weight(p, q, r):
        return w_ref[tap(p, q, r)].astype(F32)

    for n, p in enumerate((-1, 0, 1)):
        rows = []
        for r in (-1, 0, 1):
            rows.append(
                jnp.concatenate([weight(p, -1, r), weight(p, 0, r), weight(p, 1, r), none], axis=1)
            )
        rows.append(jnp.zeros((CH, 4 * CH), F32))
        wf[n * 256 : (n + 1) * 256] = jnp.concatenate(rows, axis=0).astype(BF16)
        cols = []
        for q in (0, -1, None, 1):
            if q is None:
                cols.append(jnp.zeros((CH, 4 * CH), F32))
            else:
                cols.append(
                    jnp.concatenate(
                        [weight(-p, -q, 0), weight(-p, -q, 1), none, weight(-p, -q, -1)], axis=1
                    )
                )
        wb[n * 256 : (n + 1) * 256] = jnp.concatenate(cols, axis=0).T.astype(BF16)

    gather_start(0)
    lax.fori_loop(0, 6, convolve, 0)
    gather_start(1)
    gather_start(2)
    lax.fori_loop(6, 8, convolve, 0)
    for n in range(3):
        scatter_sent_wait(n)
    pair_back_start(0)
    finish(0, 0)
    pair_back_start(1)
    pair_back_start(2)
    for n in range(3):
        gather_sent_wait(n)
    finish(1, -1)
    finish(2, 1)


def write_out(*refs):
    sems = refs[6]
    copies = [pltpu.make_async_copy(refs[n], refs[n + 3], sems.at[n]) for n in range(3)]
    for copy in copies:
        copy.start()
    for copy in copies:
        copy.wait()


def shards(cells, features, cotangent, weight, mask_words, neighbors):
    scale = float(cells * 2 * LEAVES * VOX) ** -0.5
    vmem = pltpu.VMEM
    dma = pltpu.SemaphoreType.DMA
    in_hbm = pl.BlockSpec(memory_space=pltpu.HBM)
    anywhere = pl.BlockSpec(memory_space=pl.ANY)
    field = jax.ShapeDtypeStruct((LEAVES, CH, VOX), BF16)
    results = (field, field, jax.ShapeDtypeStruct((27, CH, CH), F32))
    per = -(-18 // cells)
    groups = 18 // per
    tiles = (groups, per, 8, 128)
    made = pl.pallas_call(
        functools.partial(kernel, cells, scale),
        out_shape=results,
        in_specs=[in_hbm] * 5,
        out_specs=(pl.BlockSpec(memory_space=pltpu.VMEM),) * 3,
        scratch_shapes=[
            vmem((LEAVES, CH, VOX), BF16),
            vmem((LEAVES, CH, VOX), BF16),
            vmem((27, CH, CH), BF16),
            vmem(mask_words.shape, jnp.int32),
            pltpu.SMEM(neighbors.shape, jnp.int32),
            vmem((LEAVES, 1, VOX), F32),
            vmem((LEAVES + 1, SIDE, SIDE, SIDE, 128), F32),
            vmem((2 * LEAVES + 1, SIDE, SIDE, 128), F32),
            vmem((2 * LEAVES + 1, SIDE, SIDE, 128), F32),
            vmem((LEAVES, PLANE, 128), BF16),
            vmem((LEAVES, PLANE, 128), BF16),
            vmem((LEAVES, PLANE, 128), BF16),
            vmem((LEAVES, PLANE, 128), BF16),
            vmem((10, LEAVES, ROWS, 128), BF16),
            vmem((10, LEAVES, ROWS, 128), BF16),
            vmem((10, LEAVES, ROWS, 128), BF16),
            vmem((3 * CH, LEAVES * WIDE), BF16),
            vmem((768, 256), BF16),
            vmem((768, 256), BF16),
            vmem((256, 192), F32),
            vmem((3, 192, 256), F32),
            vmem((3, 2) + tiles, F32),
            vmem((3,) + tiles, F32),
            vmem((3,) + tiles, F32),
            vmem((3, cells) + tiles[1:], F32),
            vmem((3,) + tiles[1:], F32),
            vmem((3, 2) + tiles, F32),
            dma((5,)),
            dma((2, 2)),
            dma((4, 3)),
            dma((3,)),
            dma((3,)),
            dma((3,)),
            dma((3,)),
        ],
        compiler_params=pltpu.CompilerParams(
            collective_id=0, has_side_effects=True, vmem_limit_bytes=54_000_000
        ),
        name="sparse_conv",
    )(*(pltpu.with_memory_space_constraint(a, pltpu.HBM) for a in (features, cotangent, weight, mask_words, neighbors)))
    return pl.pallas_call(
        write_out,
        out_shape=results,
        in_specs=[anywhere] * 3,
        out_specs=(in_hbm,) * 3,
        scratch_shapes=[dma((3,))],
        compiler_params=pltpu.CompilerParams(vmem_limit_bytes=1_000_000),
        name="write_out",
    )(*made)


def solution(mesh):
    placed = (
        P(("scene", "dom"), None, None),
        P(("scene", "dom"), None, None),
        P(),
        P(("scene", "dom"), None),
        P(("scene", "dom"), None),
    )
    return jax.shard_map(
        functools.partial(shards, mesh.shape["dom"] // 2),
        mesh=mesh,
        in_specs=placed,
        out_specs=(
            P(("scene", "dom"), None, None),
            P(("scene", "dom"), None, None),
            P("scene", None, None),
        ),
        check_vma=False,
    )
```
